256 devices in a mesh: section: 8 (over z_hi, core), expert: 32 (over x, y, z_lo).
Axes of the slice: x: 4, y: 4, z: 8 (z_hi: 4, z_lo: 2; z = z_hi * 2 + z_lo), core: 2. Of those that a mesh axis runs over, the one named last changes fastest.
Arguments:
- layer_in: bfloat16 [8, 4096, 5120], P('section', 'expert'), may hold values from -50 to 50
- memory: bfloat16 [8, 128, 2, 5120], P('section', 'expert'), may hold values from -80 to 80
- cotangent: bfloat16 [8, 4096, 5120], P('section', 'expert'), may hold values from -6 to 6
- norm_gain: float32 [8, 5120], P('section'), may hold values from 0.5 to 1.5
- attn_gain: float32 [8, 5120], P('section'), may hold values from 0.5 to 1.5
- expert_in: bfloat16 [8, 5120, 10240], P('section', None, 'expert'), may hold values from -0.078125 to 0.078125
- expert_out: bfloat16 [8, 10240, 5120], P('section', 'expert'), may hold values from -0.0625 to 0.0625
- slot_index: int32 [8, 4096], P('section', 'expert'), may hold values from -1 to 7, as said below
- gate_prob: float32 [8, 4096], P('section', 'expert'), may hold values from 0.2 to 1
Outputs:
- layer_out: bfloat16 [8, 4096, 5120], P('section', 'expert')
- arriving: bfloat16 [8, 4096, 5120], P('section', 'expert')
- grad_memory: float32 [8, 128, 2, 5120], P('section', 'expert')
The draws below stay inside these ranges and needn't reach their ends.
Inputs may be any that keep to these rules, and one draw needn't show every extreme that they name: `slot_index`: within each aligned block of 128 tokens of a layer the slots used are 0 to that block's count minus 1, each once; counts lie between 8 // 3 (at least 1) and 8, and every layer has a block with all 8 slots used.
All inputs are finite; a program needn't handle non-finite values.
Results may differ from the reference program's by a relative error of at most 0.0049.
The reference program's roundings to bfloat16 on the way (of `queries`, `residual`, `normed`, `capacity` and `hidden`) count: a program that leaves them out, or rounds other values in their place, can miss the bound.
Values may be sent and summed in bfloat16 or wider, within the bound.
A program may use at most 128 MiB of HBM per device.

```python
import jax
import jax.numpy as jnp
from jax import lax

D = 5120
HD = 128
FFW = 10240
TOK_DEV = 128
MEM = 128
CAP = 8
LAYERS = 8
TOKENS = 4096


def draw_memory(key, part):
    key = jax.random.fold_in(key, 11)
    key_draw = jax.random.fold_in(key, 3)
    value_draw = jax.random.fold_in(key, 4)
    keys = jnp.clip(jax.random.normal(key_draw, (LAYERS, MEM, D), jnp.float32), -4.0, 4.0)
    values = jnp.clip(jax.random.normal(value_draw, (LAYERS, MEM, D), jnp.float32), -4.0, 4.0)
    return jnp.stack([keys, values], axis=2).astype(jnp.bfloat16)


def draw_layer_in(key, part):
    key = jax.random.fold_in(key, 23)
    base = jnp.clip(jax.random.normal(key, (LAYERS, TOKENS, D), jnp.float32), -5.0, 5.0)
    return base.astype(jnp.bfloat16)


def draw_slot_index(key, part):
    key = jax.random.fold_in(key, 37)
    groups = TOKENS // TOK_DEV
    count_key, full_key, order_key = jax.random.split(key, 3)
    counts = jax.random.randint(count_key, (LAYERS, groups), max(CAP // 3, 1), CAP + 1)
    full_at = jax.random.randint(full_key, (LAYERS,), 0, groups)
    counts = jnp.where(jnp.arange(groups, dtype=jnp.int32)[None, :] == full_at[:, None], CAP, counts)
    order_keys = jax.random.split(order_key, LAYERS * groups)
    ranks = jax.vmap(lambda single: jax.random.permutation(single, TOK_DEV))(order_keys)
    ranks = ranks.reshape(LAYERS, groups, TOK_DEV).astype(jnp.int32)
    chosen = jnp.where(ranks < counts[:, :, None], ranks, -1)
    return chosen.reshape(LAYERS, TOKENS).astype(jnp.int32)


def steps_of(rng, shape, cuts, low, top_value):
    def one(axis_at, shards_of):
        heights = jax.random.uniform(jax.random.fold_in(jax.random.fold_in(rng, 6), axis_at), (shards_of,), jnp.float32, low / len(cuts), top_value / len(cuts))
        return jnp.repeat(jnp.exp(heights), shape[axis_at] // shards_of).reshape((-1,) + (1,) * (len(shape) - axis_at - 1))

    factor_of = one(*cuts[0])
    for cut in cuts[1:]:
        factor_of = factor_of * one(*cut)
    return factor_of


def bell_draw(stream_key, dims, scale, bound, pieces=(), held_as=jnp.bfloat16):
    values = jax.random.normal(stream_key, dims, jnp.float32) * scale
    if len(pieces) > 0:
        values = steps_of(stream_key, dims, pieces, -0.22, 0.18) * values
    return jnp.clip(values, min=-bound, max=bound).astype(held_as)


def setup_inputs(seed: int = 0) -> dict:
    key_list = jax.random.split(jax.random.key(seed), 10)
    layer_in = draw_layer_in(jax.random.fold_in(key_list[9], 71), 0)
    memory = draw_memory(jax.random.fold_in(key_list[9], 71), 0)
    cotangent = bell_draw(key_list[2], (LAYERS, TOKENS, D), 1.0, 6.0, ((0, 8), (1, 32)))
    norm_gain = jnp.clip(1.0 + 0.1 * jax.random.normal(key_list[3], (LAYERS, D), jnp.float32), 0.5, 1.5)
    attn_gain = jnp.clip(1.0 + 0.1 * jax.random.normal(key_list[4], (LAYERS, D), jnp.float32), 0.5, 1.5)
    expert_in = bell_draw(key_list[5], (LAYERS, D, FFW), D ** -0.5, 0.078125, ((0, 8), (2, 32)))
    expert_out = bell_draw(key_list[6], (LAYERS, FFW, D), FFW ** -0.5, 0.0625, ((0, 8), (1, 32)))
    slot_index = draw_slot_index(jax.random.fold_in(key_list[9], 71), 0)
    gate_prob = jnp.clip(0.2 + 0.8 * jax.random.uniform(key_list[8], (LAYERS, TOKENS), jnp.float32) ** steps_of(key_list[8], (LAYERS, TOKENS), ((0, 8), (1, 32)), -0.2, 0.2), 0.2, 1.0)
    return dict(layer_in=layer_in, memory=memory, cotangent=cotangent, norm_gain=norm_gain, attn_gain=attn_gain, expert_in=expert_in, expert_out=expert_out, slot_index=slot_index, gate_prob=gate_prob)


def rms_scale(values, scale_row):
    return values * lax.rsqrt(lax.optimization_barrier(jnp.mean(values * values, axis=-1, keepdims=True)) + 1e-06) * scale_row

def attend_grad(queries, keys, values, upstream):
    query_rows = queries.shape[0]
    source_rows = keys.shape[0]
    per_head_queries = queries.reshape(query_rows, -1, HD)
    per_head_keys = keys.reshape(source_rows, -1, HD)
    per_head_values = values.reshape(source_rows, -1, HD)
    incoming_head_gradient = upstream.reshape(query_rows, -1, HD)
    scaling_factor = HD ** (-0.5)
    attention_scores = jnp.einsum('ksu,lsu->skl', per_head_queries, per_head_keys, preferred_element_type=jnp.float32) * scaling_factor
    highest = lax.optimization_barrier(jnp.max(attention_scores, axis=-1, keepdims=True))
    weights = jnp.exp(attention_scores - highest)
    weights = weights / lax.optimization_barrier(jnp.sum(weights, axis=-1, keepdims=True))
    rounded_down = weights.astype(jnp.bfloat16)
    expert_mixture = jnp.einsum('cif,fcv->icv', rounded_down, per_head_values, preferred_element_type=jnp.float32)
    value_gradient_rows = jnp.einsum('yfg,fyb->gyb', rounded_down, incoming_head_gradient, preferred_element_type=jnp.float32)
    probability_gradient = jnp.einsum('ksu,lsu->skl', incoming_head_gradient, per_head_values, preferred_element_type=jnp.float32)
    dscore = weights * (probability_gradient - lax.optimization_barrier(jnp.sum(probability_gradient * weights, axis=-1, keepdims=True))) * scaling_factor
    upper_limit = dscore.astype(jnp.bfloat16)
    lower_limit = (dscore - upper_limit.astype(jnp.float32)).astype(jnp.bfloat16)
    key_gradient_rows = jnp.einsum('yfg,fyb->gyb', upper_limit, per_head_queries, preferred_element_type=jnp.float32)
    key_gradient_rows = key_gradient_rows + jnp.einsum('yfg,fyb->gyb', lower_limit, per_head_queries, preferred_element_type=jnp.float32)
    stacked = jnp.stack([key_gradient_rows.reshape(source_rows, -1), value_gradient_rows.reshape(source_rows, -1)], axis=1)
    return (expert_mixture.reshape(query_rows, -1), stacked)

def reference(layer_in, memory, cotangent, norm_gain, attn_gain, expert_in, expert_out, slot_index, gate_prob):
    groups = TOKENS // TOK_DEV
    produced = []
    grads = []
    for section_number in range(LAYERS):
        current = layer_in[section_number].astype(jnp.float32)
        if section_number >= LAYERS // 2:
            queries = rms_scale(current, attn_gain[section_number]).astype(jnp.bfloat16)
            expert_mixture, grad_part = attend_grad(queries, memory[section_number, :, 0], memory[section_number, :, 1], cotangent[section_number])
            grads.append(grad_part)
            residual = (current + expert_mixture).astype(jnp.bfloat16)
        else:
            grads.append(jnp.zeros((MEM, 2, D), jnp.float32))
            residual = layer_in[section_number]
        normed = rms_scale(residual.astype(jnp.float32), norm_gain[section_number]).astype(jnp.bfloat16)
        onehot = slot_index[section_number].reshape(groups, 1, TOK_DEV) == jnp.arange(CAP, dtype=jnp.int32).reshape(1, CAP, 1)
        capacity = jnp.einsum('gct,gtd->gcd', onehot.astype(jnp.bfloat16), normed.reshape(groups, TOK_DEV, D), preferred_element_type=jnp.float32)
        capacity = capacity.astype(jnp.bfloat16).reshape(groups * CAP, D)
        hidden = jax.nn.gelu(jnp.dot(capacity, expert_in[section_number], preferred_element_type=jnp.float32)).astype(jnp.bfloat16)
        computed = jnp.dot(hidden, expert_out[section_number], preferred_element_type=jnp.float32)
        combined = jnp.einsum('gct,gcd->gtd', onehot.astype(jnp.float32), computed.reshape(groups, CAP, D), precision=lax.Precision.HIGHEST).reshape(TOKENS, D)
        produced.append((residual.astype(jnp.float32) + gate_prob[section_number][:, None] * combined).astype(jnp.bfloat16))
    layer_out = jnp.stack(produced)
    arriving = jnp.concatenate([jnp.zeros_like(layer_out[:1]), layer_out[:-1]], axis=0)
    return (layer_out, arriving, jnp.stack(grads))
```

```python
import jax
import jax.numpy as jnp
from jax import lax
from jax.experimental import pallas as pl
from jax.experimental.pallas import tpu as pltpu
from jax.sharding import PartitionSpec as P

HD = 128
CAP = 8
RING = 4
MESH = pl.DeviceIdType.MESH
BF = jnp.bfloat16
F32 = jnp.float32
NT = (((1,), (1,)), ((), ()))
TN = (((0,), (0,)), ((), ()))


def dot(a, b, dims=(((1,), (0,)), ((), ()))):
    return lax.dot_general(a, b, dims, preferred_element_type=F32)


class Links:
    def __init__(self, send, recv, section, x, y, z):
        self.send, self.recv = send, recv
        self.section, self.x, self.y, self.z = section, x, y, z
        self.started = []

    def copy(self, key, src, dst, device):
        return pltpu.make_async_remote_copy(
            src_ref=src,
            dst_ref=dst,
            send_sem=self.send.at[key],
            recv_sem=self.recv.at[key],
            device_id=device,
            device_id_type=MESH,
        )

    def put(self, key, src, dst, device):
        copy = self.copy(key, src, dst, device)
        copy.start()
        self.started.append(copy)

    def got(self, key, dst, device):
        self.copy(key, dst, dst, device).wait_recv()

    def finish(self):
        for copy in self.started:
            copy.wait_send()
        self.started = []


class Half:
    def __init__(self, links, first, lane, width):
        self.links, self.first, self.lane, self.width = links, first, lane, width
        self.u, self.v = (links.x, links.y) if first == "x" else (links.y, links.x)

    def at(self, buf, u, v, low=0, size=None):
        lanes = pl.ds(self.lane + low, self.width if size is None else size)
        if self.first == "x":
            return buf.at[u, v, :, :, lanes]
        return buf.at[v, u, :, :, lanes]

    def device(self, u, v):
        x, y = (u, v) if self.first == "x" else (v, u)
        return (self.links.section, x * (RING * 2) + y * 2 + self.links.z)


def step(i, by):
    return lax.rem(i + by + RING, RING)


GATHER_KEYS = 41
SCATTER_KEYS = 41


def gather(links, halves, buf, base):
    x, y, z = links.x, links.y, links.z
    pair = (links.section, x * (RING * 2) + y * 2 + (1 - z))
    links.put(base, buf.at[x, y, z], buf.at[x, y, z], pair)
    yield
    links.got(base, buf.at[x, y, 1 - z], pair)

    def spread(half, key, slot, u):
        part = half.at(buf, u, half.v)
        for turn in (1, -1):
            links.put(
                key + 4 + slot * 4 + (turn < 0),
                part,
                part,
                half.device(half.u, step(half.v, turn)),
            )

    def relay(half, key, slot, u):
        q = half.width // 2
        for turn in (1, -1):
            left = step(half.v, -turn)
            k = key + 4 + slot * 4 + (turn < 0)
            links.got(k, half.at(buf, u, left), half.device(half.u, left))
            part = half.at(buf, u, left, 0 if turn > 0 else q, q)
            links.put(k + 2, part, part, half.device(half.u, step(half.v, turn)))

    keyed = [(half, base + 1 + 20 * i) for i, half in enumerate(halves)]
    for half, key in keyed:
        part = half.at(buf, half.u, half.v)
        for turn in (1, -1):
            links.put(key + (turn < 0), part, part, half.device(step(half.u, turn), half.v))
    for half, key in keyed:
        spread(half, key, 0, half.u)
    yield
    for half, key in keyed:
        q = half.width // 2
        for slot, turn in ((1, 1), (2, -1)):
            left = step(half.u, -turn)
            links.got(key + (turn < 0), half.at(buf, left, half.v), half.device(left, half.v))
            part = half.at(buf, left, half.v, 0 if turn > 0 else q, q)
            links.put(key + 2 + (turn < 0), part, part, half.device(step(half.u, turn), half.v))
            spread(half, key, slot, left)
    yield
    for half, key in keyed:
        relay(half, key, 0, half.u)
    yield
    for half, key in keyed:
        q = half.width // 2
        far = step(half.u, 2)
        for turn in (1, -1):
            part = half.at(buf, far, half.v, 0 if turn > 0 else q, q)
            links.got(key + 2 + (turn < 0), part, half.device(step(half.u, -turn), half.v))
        spread(half, key, 3, far)
    yield
    for half, key in keyed:
        relay(half, key, 1, step(half.u, -1))
        relay(half, key, 2, step(half.u, 1))
    yield
    for half, key in keyed:
        relay(half, key, 3, step(half.u, 2))
    yield
    for half, key in keyed:
        q = half.width // 2
        for slot, by in ((0, 0), (1, -1), (2, 1), (3, 2)):
            for turn in (1, -1):
                part = half.at(
                    buf, step(half.u, by), step(half.v, 2), 0 if turn > 0 else q, q
                )
                links.got(
                    key + 4 + slot * 4 + 2 + (turn < 0),
                    part,
                    half.device(half.u, step(half.v, -turn)),
                )


def add_into(target, *others):
    total = target[...].astype(F32)
    for other in others:
        total = total + other[...].astype(F32)
    target[...] = total.astype(target.dtype)


def scatter(links, halves, buf, land, base):
    passing2, whole2, passing1, whole1, last = land
    x, y, z = links.x, links.y, links.z
    order = ((0, 2), (1, -1), (2, 1), (3, 0))
    keyed = [(i, half, base + 1 + 20 * i) for i, half in enumerate(halves)]
    for slot, by in order:
        for i, half, key in keyed:
            q = half.width // 2
            for turn in (1, -1):
                d = int(turn < 0)
                links.put(
                    key + slot * 4 + d,
                    half.at(buf, step(half.u, by), step(half.v, 2), d * q, q),
                    passing2.at[i, slot, d],
                    half.device(half.u, step(half.v, turn)),
                )
    yield
    for slot, by in order:
        for i, half, key in keyed:
            q = half.width // 2
            for turn in (1, -1):
                d = int(turn < 0)
                to = step(half.v, turn)
                links.got(
                    key + slot * 4 + d,
                    passing2.at[i, slot, d],
                    half.device(half.u, step(half.v, -turn)),
                )
                add_into(
                    half.at(buf, step(half.u, by), to, d * q, q), passing2.at[i, slot, d]
                )
                links.put(
                    key + slot * 4 + 2 + d,
                    half.at(buf, step(half.u, by), to),
                    whole2.at[i, slot, d],
                    half.device(half.u, to),
                )
        yield
    for slot, by in order:
        for i, half, key in keyed:
            q = half.width // 2
            for d, turn in ((0, 1), (1, -1)):
                links.got(
                    key + slot * 4 + 2 + d,
                    whole2.at[i, slot, d],
                    half.device(half.u, step(half.v, -turn)),
                )
            add_into(
                half.at(buf, step(half.u, by), half.v),
                whole2.at[i, slot, 0],
                whole2.at[i, slot, 1],
            )
            if by == 2:
                for d, turn in ((0, 1), (1, -1)):
                    links.put(
                        key + 16 + d,
                        half.at(buf, step(half.u, 2), half.v, d * q, q),
                        passing1.at[i, d],
                        half.device(step(half.u, turn), half.v),
                    )
            if by == 1:
                for d, turn in ((0, 1), (1, -1)):
                    to = step(half.u, turn)
                    links.got(
                        key + 16 + d, passing1.at[i, d], half.device(step(half.u, -turn), half.v)
                    )
                    add_into(half.at(buf, to, half.v, d * q, q), passing1.at[i, d])
                    links.put(
                        key + 18 + d,
                        half.at(buf, to, half.v),
                        whole1.at[i, d],
                        half.device(to, half.v),
                    )
        yield
    for i, half, key in keyed:
        for d, turn in ((0, 1), (1, -1)):
            links.got(key + 18 + d, whole1.at[i, d], half.device(step(half.u, -turn), half.v))
        add_into(half.at(buf, half.u, half.v), whole1.at[i, 0], whole1.at[i, 1])
    pair = (links.section, x * (RING * 2) + y * 2 + (1 - z))
    links.put(base, buf.at[x, y, 1 - z], last, pair)
    yield
    links.got(base, last, pair)


def drive(streams, tasks=()):
    streams, tasks = list(streams), list(tasks)
    while streams or tasks:
        for stream in list(streams):
            if next(stream, "end") == "end":
                streams.remove(stream)
        if tasks:
            tasks.pop(0)()


def scaled(rows, gain):
    return rows * lax.rsqrt(jnp.mean(rows * rows, axis=-1, keepdims=True) + 1e-06) * gain


def kernel(
    sections,
    mem_ref,
    layer_ref,
    cot_ref,
    norm_ref,
    attn_ref,
    in_ref,
    out_ref,
    slot_ref,
    gate_ref,
    layer_out,
    arriving,
    grad_out,
    cur,
    cot,
    win,
    wout,
    queries,
    resid,
    before,
    gkv,
    keys,
    values,
    gcap,
    probs,
    parts,
    gparts,
    dkeys,
    dvalues,
    picked,
    pickedq,
    attended,
    perm,
    perm_t,
    hacc,
    hidden,
    own_slot,
    their_slot,
    own_rows,
    their_rows,
    land_a,
    land_b,
    land_c,
    land_d,
    land_e,
    glast,
    gland_a,
    gland_b,
    gland_c,
    gland_d,
    load_sem,
    send_sem,
    recv_sem,
):
    tokens, width = cur.shape
    half_width = width // 2
    heads = width // HD
    ffw = win.shape[1]
    scaling_factor = HD ** (-0.5)
    section = lax.axis_index("section")
    place = lax.axis_index("expert")
    x, y, z = place // (RING * 2), (place // 2) % RING, place % 2
    links = Links(send_sem, recv_sem, section, x, y, z)
    halves = (
        Half(links, "x", 0, half_width // 2),
        Half(links, "y", half_width // 2, half_width // 2),
    )
    cap_base, kv_base = 0, GATHER_KEYS
    ret_base = kv_base + GATHER_KEYS
    grad_base = ret_base + SCATTER_KEYS
    pass_base = grad_base + SCATTER_KEYS

    loads = [
        pltpu.make_async_copy(src, dst, load_sem.at[i])
        for i, (src, dst) in enumerate(
            ((layer_ref, cur), (cot_ref, cot), (in_ref, win), (out_ref, wout))
        )
    ]
    for load in loads:
        load.start()

    def device(xx, yy, zz):
        return (section, xx * (RING * 2) + yy * 2 + zz)

    barrier = pltpu.get_barrier_semaphore()
    for peer in (
        device(x, y, 1 - z),
        device(step(x, 1), y, z),
        device(step(x, -1), y, z),
        device(x, step(y, 1), z),
        device(x, step(y, -1), z),
    ):
        pl.semaphore_signal(barrier, inc=1, device_id=peer, device_id_type=MESH)

    @pl.when(section > 0)
    def _():
        pl.semaphore_signal(
            barrier, inc=1, device_id=(section - 1, place), device_id_type=MESH
        )

    @pl.when(section < sections - 1)
    def _():
        pl.semaphore_signal(
            barrier, inc=1, device_id=(section + 1, place), device_id_type=MESH
        )

    ends = jnp.where(section > 0, 1, 0) + jnp.where(section < sections - 1, 1, 0)
    pl.semaphore_wait(barrier, 5 + ends)

    def pass_copy(key, src, dst):
        return links.copy(pass_base + key, src, dst, (section + 1, place))

    def pass_on(key, src, dst):
        @pl.when(section < sections - 1)
        def _():
            pass_copy(key, src, dst).start()

    def pass_sent(key, src, dst):
        @pl.when(section < sections - 1)
        def _():
            pass_copy(key, src, dst).wait_send()

    def pass_got(key, dst):
        @pl.when(section > 0)
        def _():
            links.copy(pass_base + key, dst, dst, (section - 1, place)).wait_recv()

    slots = slot_ref[...]
    rows16 = lax.broadcasted_iota(jnp.int32, (2 * CAP, tokens), 0)
    onehot = (slots == rows16).astype(F32).astype(BF)
    has_row = jnp.sum((slots == rows16).astype(F32), axis=-1, keepdims=True)

    def pick(source, target):
        def one(i, carry):
            lanes = pl.ds(pl.multiple_of(i * 512, 512), 512)
            target[:, lanes] = dot(onehot, source[:, lanes]).astype(target.dtype)
            return carry

        lax.fori_loop(0, width // 512, one, 0)

    def fold(rows):
        return jnp.concatenate([rows[:CAP, :half_width], rows[:CAP, half_width:]], axis=0)

    def put_capacity():
        rows = picked[...].astype(F32)
        gcap[x, y, z] = fold(scaled(rows, norm_ref[...])).astype(BF)

    def expert():
        loads[2].wait()
        loads[3].wait()
        hacc[...] = jnp.zeros_like(hacc)

        def into(k, carry):
            lanes = pl.ds(pl.multiple_of(k * 256, 256), 256)
            block = gcap[:, :, :, :, lanes].reshape(-1, 256)
            low = dot(block, win[lanes, :])
            high_rows = pl.ds(pl.multiple_of(half_width + k * 256, 256), 256)
            high = dot(block, win[high_rows, :])
            low = low.reshape(-1, 2 * CAP, ffw)[:, :CAP]
            high = high.reshape(-1, 2 * CAP, ffw)[:, CAP:]
            hacc[...] += low + high
            return carry

        lax.fori_loop(0, half_width // 256, into, 0)
        hidden[...] = jax.nn.gelu(hacc[...].reshape(-1, ffw)).astype(BF)

        def out(k, carry):
            lanes = pl.ds(pl.multiple_of(k * 256, 256), 256)
            high_lanes = pl.ds(pl.multiple_of(half_width + k * 256, 256), 256)
            low = dot(hidden[...], wout[:, lanes]).reshape(-1, CAP, 256)
            high = dot(hidden[...], wout[:, high_lanes]).reshape(-1, CAP, 256)
            block = jnp.concatenate([low, high], axis=1).astype(BF)
            parts[:, :, :, :, lanes] = block.reshape(RING, RING, 2, 2 * CAP, 256)
            return carry

        lax.fori_loop(0, half_width // 256, out, 0)

    ret_land = (land_a, land_b, land_c, land_d, land_e)

    def spread_rows(slot_rows, rows, base, target):
        lane_rows = lax.broadcasted_iota(jnp.int32, (2 * CAP, tokens), 0)
        low = (slot_rows == lane_rows).astype(F32).astype(BF)
        high = (slot_rows == lane_rows - CAP).astype(F32)
        high = jnp.where(lane_rows < CAP, 0.0, high).astype(BF)
        has = dot(low, jnp.ones((2 * CAP, 128), BF), TN)[:, :1] > 0.5
        for chosen, start in ((low, 0), (high, half_width)):

            def one(i, carry, chosen=chosen, start=start):
                lanes = pl.ds(pl.multiple_of(i * 512, 512), 512)
                full = pl.ds(pl.multiple_of(start + i * 512, 512), 512)
                moved = dot(chosen, rows[:, lanes], TN)
                kept = base[:, full].astype(F32)
                target[:, full] = jnp.where(has, moved, kept).astype(BF)
                return carry

            lax.fori_loop(0, half_width // 512, one, 0)

    def finish(base):
        returned = parts[x, y, z].astype(F32) + land_e[...].astype(F32)
        gates = jnp.sum(
            jnp.where(slots == rows16[:CAP], gate_ref[...], 0.0), axis=-1, keepdims=True
        )
        gates = jnp.concatenate([gates, gates], axis=0)
        own_rows[...] = (fold(picked[...].astype(F32)) + gates * returned).astype(BF)
        pass_on(2, own_rows, their_rows)
        spread_rows(slots, own_rows, base, layer_out)
        pass_got(0, before)
        pass_got(1, their_slot)
        pass_got(2, their_rows)

        @pl.when(section > 0)
        def _():
            spread_rows(their_slot[:1, :], their_rows, before, arriving)

        @pl.when(section == 0)
        def _():
            arriving[...] = jnp.zeros_like(arriving)

        pass_sent(0, base, before)
        pass_sent(1, own_slot, their_slot)
        pass_sent(2, own_rows, their_rows)

    own_slot[...] = jnp.broadcast_to(slots, own_slot.shape)

    @pl.when(section < sections // 2)
    def _():
        loads[0].wait()
        pick(cur, picked)
        put_capacity()
        stream = gather(links, halves, gcap, cap_base)
        next(stream)
        pass_on(0, cur, before)
        pass_on(1, own_slot, their_slot)
        drive([stream])
        loads[1].wait()
        expert()
        drive([scatter(links, halves, parts, ret_land, ret_base)])
        grad_out[...] = jnp.zeros_like(grad_out)
        finish(cur)
        links.finish()

    @pl.when(section >= sections // 2)
    def _():
        gkv[x, y, z] = mem_ref[...]

        def make_perm():
            for target, flip in ((perm, 0), (perm_t, 1)):
                k = lax.broadcasted_iota(jnp.int32, (256, 256), flip)
                i = lax.broadcasted_iota(jnp.int32, (256, 256), 1 - flip)
                m = k & 63
                source = ((m >> 2) << 4) + ((k >> 7) << 3) + ((m & 3) << 1) + ((k >> 6) & 1)
                target[...] = (source == i).astype(F32).astype(BF)

        def make_queries():
            loads[0].wait()

            def one(i, carry):
                rows = pl.ds(pl.multiple_of(i * 16, 16), 16)
                queries[rows, :] = scaled(cur[rows, :].astype(F32), attn_ref[...]).astype(BF)
                return carry

            lax.fori_loop(0, tokens // 16, one, 0)

        def pick_rows():
            pick(cur, picked)
            pick(queries, pickedq)

        drive(
            [gather(links, halves, gkv, kv_base)],
            [lambda: pass_on(1, own_slot, their_slot), make_perm, make_queries, pick_rows],
        )

        for c in range(2):

            def sort_in(i, carry, c=c):
                lanes = pl.ds(pl.multiple_of(i * 256, 256), 256)
                high = pl.ds(pl.multiple_of(half_width + i * 256, 256), 256)
                block = gkv[2 * c : 2 * c + 2, :, :, :, lanes].reshape(256, 256)
                block = dot(perm[...], block).astype(BF)
                keys[64 * c : 64 * c + 64, lanes] = block[:64]
                values[64 * c : 64 * c + 64, lanes] = block[64:128]
                keys[64 * c : 64 * c + 64, high] = block[128:192]
                values[64 * c : 64 * c + 64, high] = block[192:]
                return carry

            lax.fori_loop(0, half_width // 256, sort_in, 0)

        def chosen_heads(group, carry):
            for j in range(4):
                lanes = pl.ds(pl.multiple_of((group * 4 + j) * HD, HD), HD)
                scores = dot(pickedq[:, lanes], keys[:, lanes], NT) * scaling_factor
                weights = jnp.exp(scores - jnp.max(scores, axis=-1, keepdims=True))
                weights = weights / jnp.sum(weights, axis=-1, keepdims=True)
                mixed = dot(weights.astype(BF), values[:, lanes])
                attended[:, lanes] = picked[:, lanes].astype(F32) + mixed * has_row
            return carry

        lax.fori_loop(0, heads // 4, chosen_heads, 0)
        picked[...] = attended[...].astype(BF)
        put_capacity()

        def forward(group, carry):
            for j in range(4):
                head = group * 4 + j
                lanes = pl.ds(pl.multiple_of(head * HD, HD), HD)
                scores = dot(keys[:, lanes], queries[:, lanes], NT) * scaling_factor
                weights = jnp.exp(scores - jnp.max(scores, axis=0, keepdims=True))
                weights = weights / jnp.sum(weights, axis=0, keepdims=True)
                probs[head] = weights
                mixed = dot(weights.astype(BF), values[:, lanes], TN)
                resid[:, lanes] = (cur[:, lanes].astype(F32) + mixed).astype(BF)
            return carry

        def backward(group, carry):
            for j in range(4):
                head = group * 4 + j
                lanes = pl.ds(pl.multiple_of(head * HD, HD), HD)
                weights = probs[head]
                upstream = cot[:, lanes]
                asked = queries[:, lanes]
                dweights = dot(values[:, lanes], upstream, NT)
                inner = jnp.sum(dweights * weights, axis=0, keepdims=True)
                dscores = weights * (dweights - inner) * scaling_factor
                high = dscores.astype(BF)
                low = (dscores - high.astype(F32)).astype(BF)
                dkeys[:, lanes] = dot(
                    jnp.concatenate([high, low], axis=1),
                    jnp.concatenate([asked, asked], axis=0),
                ).astype(BF)
                dvalues[:, lanes] = dot(weights.astype(BF), upstream).astype(BF)
            return carry

        def part_of(work, i, of):
            count = heads // 4

            def task():
                lax.fori_loop(count * i // of, count * (i + 1) // of, work, 0)

            return task

        def hand_over():
            pass_on(0, resid, before)
            loads[1].wait()

        drive(
            [gather(links, halves, gcap, cap_base)],
            [part_of(forward, i, 4) for i in range(4)]
            + [hand_over]
            + [part_of(backward, i, 4) for i in range(4)],
        )

        for c in range(2):

            def sort_out(i, carry, c=c):
                lanes = pl.ds(pl.multiple_of(i * 256, 256), 256)
                high = pl.ds(pl.multiple_of(half_width + i * 256, 256), 256)
                rows = slice(64 * c, 64 * c + 64)
                block = jnp.concatenate(
                    [dkeys[rows, lanes], dvalues[rows, lanes], dkeys[rows, high], dvalues[rows, high]],
                    axis=0,
                )
                block = dot(perm_t[...], block).astype(BF)
                gparts[2 * c : 2 * c + 2, :, :, :, lanes] = block.reshape(
                    2, RING, 2, 2 * CAP, 256
                )
                return carry

            lax.fori_loop(0, half_width // 256, sort_out, 0)

        grad_stream = scatter(
            links, halves, gparts, (gland_a, gland_b, gland_c, gland_d, glast), grad_base
        )
        next(grad_stream)
        expert()
        drive([scatter(links, halves, parts, ret_land, ret_base), grad_stream])
        total = gparts[x, y, z].astype(F32) + glast[...].astype(F32)
        grad_out[...] = jnp.concatenate([total[:CAP], total[CAP:]], axis=1)
        finish(resid)
        links.finish()


def local(
    layer_in, memory, cotangent, norm_gain, attn_gain, expert_in, expert_out, slot_index, gate_prob
):
    sections = lax.axis_size("section")
    tokens, width = layer_in.shape[1:]
    rows = memory.shape[1]
    stash = rows * 2 * RING * RING
    ffw = expert_in.shape[2]
    half = width // 2
    heads = width // HD
    mem = memory[0].reshape(rows * 2, 2, half).transpose(1, 0, 2).reshape(rows * 4, half)
    vmem = pl.BlockSpec(memory_space=pltpu.VMEM)
    anywhere = pl.BlockSpec(memory_space=pl.ANY)
    full = (RING, RING, 2, 2 * CAP, half)
    quarter = half // 4
    landing = [
        pltpu.VMEM((2, RING, 2, 2, 2 * CAP, quarter), BF),
        pltpu.VMEM((2, RING, 2, 2, 2 * CAP, 2 * quarter), BF),
        pltpu.VMEM((2, 2, 2, 2 * CAP, quarter), BF),
        pltpu.VMEM((2, 2, 2, 2 * CAP, 2 * quarter), BF),
    ]
    count = 2 * GATHER_KEYS + 2 * SCATTER_KEYS + 3
    layer_out, arriving, grad = pl.pallas_call(
        lambda *refs: kernel(sections, *refs),
        out_shape=(
            jax.ShapeDtypeStruct((tokens, width), BF),
            jax.ShapeDtypeStruct((tokens, width), BF),
            jax.ShapeDtypeStruct((rows * 2, width), F32),
        ),
        in_specs=[vmem, anywhere, anywhere, vmem, vmem, anywhere, anywhere, vmem, vmem],
        out_specs=(vmem, vmem, vmem),
        scratch_shapes=[
            pltpu.VMEM((tokens, width), BF),
            pltpu.VMEM((tokens, width), BF),
            pltpu.VMEM((width, ffw), BF),
            pltpu.VMEM((ffw, width), BF),
            pltpu.VMEM((tokens, width), BF),
            pltpu.VMEM((tokens, width), BF),
            pltpu.VMEM((tokens, width), BF),
            pltpu.VMEM(full, BF),
            pltpu.VMEM((stash, width), BF),
            pltpu.VMEM((stash, width), BF),
            pltpu.VMEM(full, BF),
            pltpu.VMEM((heads, stash, tokens), F32),
            pltpu.VMEM(full, BF),
            pltpu.VMEM(full, BF),
            pltpu.VMEM((stash, width), BF),
            pltpu.VMEM((stash, width), BF),
            pltpu.VMEM((2 * CAP, width), BF),
            pltpu.VMEM((2 * CAP, width), BF),
            pltpu.VMEM((2 * CAP, width), F32),
            pltpu.VMEM((256, 256), BF),
            pltpu.VMEM((256, 256), BF),
            pltpu.VMEM((2 * RING * RING, CAP, ffw), F32),
            pltpu.VMEM((2 * RING * RING * CAP, ffw), BF),
            pltpu.VMEM((8, tokens), jnp.int32),
            pltpu.VMEM((8, tokens), jnp.int32),
            pltpu.VMEM((2 * CAP, half), BF),
            pltpu.VMEM((2 * CAP, half), BF),
            *landing,
            pltpu.VMEM((2 * CAP, half), BF),
            pltpu.VMEM((2 * CAP, half), BF),
            *landing,
            pltpu.SemaphoreType.DMA((4,)),
            pltpu.SemaphoreType.DMA((count,)),
            pltpu.SemaphoreType.DMA((count,)),
        ],
        compiler_params=pltpu.CompilerParams(
            collective_id=0, has_side_effects=True, vmem_limit_bytes=60 * 1024 * 1024
        ),
    )(
        mem,
        layer_in[0],
        cotangent[0],
        norm_gain,
        attn_gain,
        expert_in[0],
        expert_out[0],
        slot_index,
        gate_prob,
    )
    return (layer_out[None], arriving[None], grad.reshape(1, rows, 2, width))


def solution(mesh):
    placed = (
        P("section", "expert", None),
        P("section", "expert", None, None),
        P("section", "expert", None),
        P("section", None),
        P("section", None),
        P("section", None, "expert"),
        P("section", "expert", None),
        P("section", "expert"),
        P("section", "expert"),
    )
    return jax.shard_map(
        local,
        mesh=mesh,
        in_specs=placed,
        out_specs=(
            P("section", "expert", None),
            P("section", "expert", None),
            P("section", "expert", None, None),
        ),
        check_vma=False,
    )
```

```python
import jax
import jax.numpy as jnp
from jax import lax
from jax.experimental import pallas as pl
from jax.experimental.pallas import tpu as pltpu
from jax.sharding import PartitionSpec as P

HD = 128
CAP = 8
RING = 4
MESH = pl.DeviceIdType.MESH
BF = jnp.bfloat16
F32 = jnp.float32
NT = (((1,), (1,)), ((), ()))
TN = (((0,), (0,)), ((), ()))


def dot(a, b, dims=(((1,), (0,)), ((), ()))):
    return lax.dot_general(a, b, dims, preferred_element_type=F32)


class Links:
    def __init__(self, send, recv, section, x, y, z):
        self.send, self.recv = send, recv
        self.section, self.x, self.y, self.z = section, x, y, z
        self.started = []

    def copy(self, key, src, dst, device):
        return pltpu.make_async_remote_copy(
            src_ref=src,
            dst_ref=dst,
            send_sem=self.send.at[key],
            recv_sem=self.recv.at[key],
            device_id=device,
            device_id_type=MESH,
        )

    def put(self, key, src, dst, device):
        copy = self.copy(key, src, dst, device)
        copy.start()
        self.started.append(copy)

    def got(self, key, dst, device):
        self.copy(key, dst, dst, device).wait_recv()

    def finish(self):
        for copy in self.started:
            copy.wait_send()
        self.started = []


class Half:
    def __init__(self, links, first, lane, width):
        self.links, self.first, self.lane, self.width = links, first, lane, width
        self.u, self.v = (links.x, links.y) if first == "x" else (links.y, links.x)

    def at(self, buf, u, v, low=0, size=None):
        lanes = pl.ds(self.lane + low, self.width if size is None else size)
        if self.first == "x":
            return buf.at[u, v, :, :, lanes]
        return buf.at[v, u, :, :, lanes]

    def device(self, u, v):
        x, y = (u, v) if self.first == "x" else (v, u)
        return (self.links.section, x * (RING * 2) + y * 2 + self.links.z)


def step(i, by):
    return lax.rem(i + by + RING, RING)


GATHER_KEYS = 41
SCATTER_KEYS = 41


def gather(links, halves, buf, base):
    x, y, z = links.x, links.y, links.z
    pair = (links.section, x * (RING * 2) + y * 2 + (1 - z))
    links.put(base, buf.at[x, y, z], buf.at[x, y, z], pair)
    yield
    links.got(base, buf.at[x, y, 1 - z], pair)

    def spread(half, key, slot, u):
        part = half.at(buf, u, half.v)
        for turn in (1, -1):
            links.put(
                key + 4 + slot * 4 + (turn < 0),
                part,
                part,
                half.device(half.u, step(half.v, turn)),
            )

    def relay(half, key, slot, u):
        q = half.width // 2
        for turn in (1, -1):
            left = step(half.v, -turn)
            k = key + 4 + slot * 4 + (turn < 0)
            links.got(k, half.at(buf, u, left), half.device(half.u, left))
            part = half.at(buf, u, left, 0 if turn > 0 else q, q)
            links.put(k + 2, part, part, half.device(half.u, step(half.v, turn)))

    keyed = [(half, base + 1 + 20 * i) for i, half in enumerate(halves)]
    for half, key in keyed:
        part = half.at(buf, half.u, half.v)
        for turn in (1, -1):
            links.put(key + (turn < 0), part, part, half.device(step(half.u, turn), half.v))
    for half, key in keyed:
        spread(half, key, 0, half.u)
    yield
    for half, key in keyed:
        q = half.width // 2
        for slot, turn in ((1, 1), (2, -1)):
            left = step(half.u, -turn)
            links.got(key + (turn < 0), half.at(buf, left, half.v), half.device(left, half.v))
            part = half.at(buf, left, half.v, 0 if turn > 0 else q, q)
            links.put(key + 2 + (turn < 0), part, part, half.device(step(half.u, turn), half.v))
            spread(half, key, slot, left)
    yield
    for half, key in keyed:
        relay(half, key, 0, half.u)
    yield
    for half, key in keyed:
        q = half.width // 2
        far = step(half.u, 2)
        for turn in (1, -1):
            part = half.at(buf, far, half.v, 0 if turn > 0 else q, q)
            links.got(key + 2 + (turn < 0), part, half.device(step(half.u, -turn), half.v))
        spread(half, key, 3, far)
    yield
    for half, key in keyed:
        relay(half, key, 1, step(half.u, -1))
        relay(half, key, 2, step(half.u, 1))
    yield
    for half, key in keyed:
        relay(half, key, 3, step(half.u, 2))
    yield
    for half, key in keyed:
        q = half.width // 2
        for slot, by in ((0, 0), (1, -1), (2, 1), (3, 2)):
            for turn in (1, -1):
                part = half.at(
                    buf, step(half.u, by), step(half.v, 2), 0 if turn > 0 else q, q
                )
                links.got(
                    key + 4 + slot * 4 + 2 + (turn < 0),
                    part,
                    half.device(half.u, step(half.v, -turn)),
                )


def add_into(target, *others):
    total = target[...].astype(F32)
    for other in others:
        total = total + other[...].astype(F32)
    target[...] = total.astype(target.dtype)


def scatter(links, halves, buf, land, base):
    passing2, whole2, passing1, whole1, last = land
    x, y, z = links.x, links.y, links.z
    order = ((0, 2), (1, -1), (2, 1), (3, 0))
    keyed = [(i, half, base + 1 + 20 * i) for i, half in enumerate(halves)]
    for slot, by in order:
        for i, half, key in keyed:
            q = half.width // 2
            for turn in (1, -1):
                d = int(turn < 0)
                links.put(
                    key + slot * 4 + d,
                    half.at(buf, step(half.u, by), step(half.v, 2), d * q, q),
                    passing2.at[i, slot, d],
                    half.device(half.u, step(half.v, turn)),
                )
    yield
    for slot, by in order:
        for i, half, key in keyed:
            q = half.width // 2
            for turn in (1, -1):
                d = int(turn < 0)
                to = step(half.v, turn)
                links.got(
                    key + slot * 4 + d,
                    passing2.at[i, slot, d],
                    half.device(half.u, step(half.v, -turn)),
                )
                add_into(
                    half.at(buf, step(half.u, by), to, d * q, q), passing2.at[i, slot, d]
                )
                links.put(
                    key + slot * 4 + 2 + d,
                    half.at(buf, step(half.u, by), to),
                    whole2.at[i, slot, d],
                    half.device(half.u, to),
                )
        yield
    for slot, by in order:
        for i, half, key in keyed:
            q = half.width // 2
            for d, turn in ((0, 1), (1, -1)):
                links.got(
                    key + slot * 4 + 2 + d,
                    whole2.at[i, slot, d],
                    half.device(half.u, step(half.v, -turn)),
                )
            add_into(
                half.at(buf, step(half.u, by), half.v),
                whole2.at[i, slot, 0],
                whole2.at[i, slot, 1],
            )
            if by == 2:
                for d, turn in ((0, 1), (1, -1)):
                    links.put(
                        key + 16 + d,
                        half.at(buf, step(half.u, 2), half.v, d * q, q),
                        passing1.at[i, d],
                        half.device(step(half.u, turn), half.v),
                    )
            if by == 1:
                for d, turn in ((0, 1), (1, -1)):
                    to = step(half.u, turn)
                    links.got(
                        key + 16 + d, passing1.at[i, d], half.device(step(half.u, -turn), half.v)
                    )
                    add_into(half.at(buf, to, half.v, d * q, q), passing1.at[i, d])
                    links.put(
                        key + 18 + d,
                        half.at(buf, to, half.v),
                        whole1.at[i, d],
                        half.device(to, half.v),
                    )
        yield
    for i, half, key in keyed:
        for d, turn in ((0, 1), (1, -1)):
            links.got(key + 18 + d, whole1.at[i, d], half.device(step(half.u, -turn), half.v))
        add_into(half.at(buf, half.u, half.v), whole1.at[i, 0], whole1.at[i, 1])
    pair = (links.section, x * (RING * 2) + y * 2 + (1 - z))
    links.put(base, buf.at[x, y, 1 - z], last, pair)
    yield
    links.got(base, last, pair)


def drive(streams, tasks=()):
    streams, tasks = list(streams), list(tasks)
    while streams or tasks:
        for stream in list(streams):
            if next(stream, "end") == "end":
                streams.remove(stream)
        if tasks:
            tasks.pop(0)()


def scaled(rows, gain):
    return rows * lax.rsqrt(jnp.mean(rows * rows, axis=-1, keepdims=True) + 1e-06) * gain


def kernel(
    sections,
    mem_ref,
    layer_ref,
    cot_ref,
    norm_ref,
    attn_ref,
    in_ref,
    out_ref,
    slot_ref,
    gate_ref,
    base_out,
    before,
    own_rows,
    their_rows,
    their_slot,
    grad_out,
    cur,
    cot,
    win,
    wout,
    queries,
    resid,
    gkv,
    keys,
    values,
    gcap,
    probs,
    parts,
    gparts,
    dkeys,
    dvalues,
    picked,
    pickedq,
    attended,
    perm,
    perm_t,
    hacc,
    hidden,
    own_slot,
    land_a,
    land_b,
    land_c,
    land_d,
    land_e,
    glast,
    gland_a,
    gland_b,
    gland_c,
    gland_d,
    load_sem,
    send_sem,
    recv_sem,
):
    tokens, width = cur.shape
    half_width = width // 2
    heads = width // HD
    ffw = win.shape[0]
    scaling_factor = HD ** (-0.5)
    section = lax.axis_index("section")
    place = lax.axis_index("expert")
    x, y, z = place // (RING * 2), (place // 2) % RING, place % 2
    links = Links(send_sem, recv_sem, section, x, y, z)
    halves = (
        Half(links, "x", 0, half_width // 2),
        Half(links, "y", half_width // 2, half_width // 2),
    )
    cap_base, kv_base = 0, GATHER_KEYS
    ret_base = kv_base + GATHER_KEYS
    grad_base = ret_base + SCATTER_KEYS
    pass_base = grad_base + SCATTER_KEYS

    loads = [
        pltpu.make_async_copy(src, dst, load_sem.at[i])
        for i, (src, dst) in enumerate(
            ((layer_ref, cur), (cot_ref, cot), (in_ref, win), (out_ref, wout))
        )
    ]
    for load in loads:
        load.start()

    def device(xx, yy, zz):
        return (section, xx * (RING * 2) + yy * 2 + zz)

    barrier = pltpu.get_barrier_semaphore()
    for peer in (
        device(x, y, 1 - z),
        device(step(x, 1), y, z),
        device(step(x, -1), y, z),
        device(x, step(y, 1), z),
        device(x, step(y, -1), z),
    ):
        pl.semaphore_signal(barrier, inc=1, device_id=peer, device_id_type=MESH)

    @pl.when(section > 0)
    def _():
        pl.semaphore_signal(
            barrier, inc=1, device_id=(section - 1, place), device_id_type=MESH
        )

    @pl.when(section < sections - 1)
    def _():
        pl.semaphore_signal(
            barrier, inc=1, device_id=(section + 1, place), device_id_type=MESH
        )

    ends = jnp.where(section > 0, 1, 0) + jnp.where(section < sections - 1, 1, 0)
    pl.semaphore_wait(barrier, 5 + ends)

    def pass_copy(key, src, dst):
        return links.copy(pass_base + key, src, dst, (section + 1, place))

    def pass_on(key, src, dst):
        @pl.when(section < sections - 1)
        def _():
            pass_copy(key, src, dst).start()

    def pass_sent(key, src, dst):
        @pl.when(section < sections - 1)
        def _():
            pass_copy(key, src, dst).wait_send()

    def pass_got(key, dst):
        @pl.when(section > 0)
        def _():
            links.copy(pass_base + key, dst, dst, (section - 1, place)).wait_recv()

    slots = slot_ref[...]
    rows16 = lax.broadcasted_iota(jnp.int32, (2 * CAP, tokens), 0)
    onehot = (slots == rows16).astype(F32).astype(BF)
    has_row = jnp.sum((slots == rows16).astype(F32), axis=-1, keepdims=True)

    def pick(source, target):
        def one(i, carry):
            lanes = pl.ds(pl.multiple_of(i * 512, 512), 512)
            target[:, lanes] = dot(onehot, source[:, lanes]).astype(target.dtype)
            return carry

        lax.fori_loop(0, width // 512, one, 0)

    def fold(rows):
        return jnp.concatenate([rows[:CAP, :half_width], rows[:CAP, half_width:]], axis=0)

    def put_capacity():
        rows = picked[...].astype(F32)
        gcap[x, y, z] = fold(scaled(rows, norm_ref[...])).astype(BF)

    def expert():
        loads[2].wait()
        loads[3].wait()
        hacc[...] = jnp.zeros_like(hacc)

        def into(k, carry):
            lanes = pl.ds(pl.multiple_of(k * 256, 256), 256)
            block = gcap[:, :, :, :, lanes].reshape(-1, 256)
            high_lanes = pl.ds(pl.multiple_of(half_width + k * 256, 256), 256)
            low = dot(block, win[:, lanes], NT)
            high = dot(block, win[:, high_lanes], NT)
            low = low.reshape(-1, 2 * CAP, ffw)[:, :CAP]
            high = high.reshape(-1, 2 * CAP, ffw)[:, CAP:]
            hacc[...] += low + high
            return carry

        lax.fori_loop(0, half_width // 256, into, 0)
        hidden[...] = jax.nn.gelu(hacc[...].reshape(-1, ffw)).astype(BF)

        def out(k, carry):
            lanes = pl.ds(pl.multiple_of(k * 256, 256), 256)
            high_lanes = pl.ds(pl.multiple_of(half_width + k * 256, 256), 256)
            low = dot(hidden[...], wout[:, lanes]).reshape(-1, CAP, 256)
            high = dot(hidden[...], wout[:, high_lanes]).reshape(-1, CAP, 256)
            block = jnp.concatenate([low, high], axis=1).astype(BF)
            parts[:, :, :, :, lanes] = block.reshape(RING, RING, 2, 2 * CAP, 256)
            return carry

        lax.fori_loop(0, half_width // 256, out, 0)

    ret_land = (land_a, land_b, land_c, land_d, land_e)

    def finish(base):
        returned = parts[x, y, z].astype(F32) + land_e[...].astype(F32)
        gates = jnp.sum(
            jnp.where(slots == rows16[:CAP], gate_ref[...], 0.0), axis=-1, keepdims=True
        )
        gates = jnp.concatenate([gates, gates], axis=0)
        own_rows[...] = (fold(picked[...].astype(F32)) + gates * returned).astype(BF)
        pass_on(2, own_rows, their_rows)
        pass_got(0, before)
        pass_got(1, their_slot)
        pass_got(2, their_rows)

        pass_sent(0, base, before)
        pass_sent(1, own_slot, their_slot)
        pass_sent(2, own_rows, their_rows)

    own_slot[...] = jnp.broadcast_to(slots, own_slot.shape)
    nothing = pltpu.make_async_copy(resid, before, load_sem.at[5])

    def keep(base):
        return pltpu.make_async_copy(base, base_out, load_sem.at[4])

    @pl.when(section < sections // 2)
    def _():
        loads[0].wait()
        pick(cur, picked)
        put_capacity()
        stream = gather(links, halves, gcap, cap_base)
        next(stream)
        pass_on(0, cur, before)
        pass_on(1, own_slot, their_slot)
        keep(cur).start()

        @pl.when(section == 0)
        def _():
            resid[...] = jnp.zeros_like(resid)
            nothing.start()
            their_slot[...] = jnp.full_like(their_slot, -1)
            their_rows[...] = jnp.zeros_like(their_rows)

        drive([stream])
        loads[1].wait()
        expert()
        drive([scatter(links, halves, parts, ret_land, ret_base)])
        grad_out[...] = jnp.zeros_like(grad_out)
        finish(cur)
        keep(cur).wait()

        @pl.when(section == 0)
        def _():
            nothing.wait()

        links.finish()

    @pl.when(section >= sections // 2)
    def _():
        rows = [mem_ref[r].astype(F32) for r in range(mem_ref.shape[0])]
        gkv[x, y, z] = fold(jnp.concatenate(rows, axis=0)).astype(BF)

        def make_perm():
            for target, flip in ((perm, 0), (perm_t, 1)):
                k = lax.broadcasted_iota(jnp.int32, (256, 256), flip)
                i = lax.broadcasted_iota(jnp.int32, (256, 256), 1 - flip)
                m = k & 63
                source = ((m >> 2) << 4) + ((k >> 7) << 3) + ((m & 3) << 1) + ((k >> 6) & 1)
                target[...] = (source == i).astype(F32).astype(BF)

        def make_queries():
            loads[0].wait()

            def one(i, carry):
                rows = pl.ds(pl.multiple_of(i * 16, 16), 16)
                queries[rows, :] = scaled(cur[rows, :].astype(F32), attn_ref[...]).astype(BF)
                return carry

            lax.fori_loop(0, tokens // 16, one, 0)

        def pick_rows():
            pick(cur, picked)
            pick(queries, pickedq)

        drive(
            [gather(links, halves, gkv, kv_base)],
            [lambda: pass_on(1, own_slot, their_slot), make_perm, make_queries, pick_rows],
        )

        for c in range(2):

            def sort_in(i, carry, c=c):
                lanes = pl.ds(pl.multiple_of(i * 256, 256), 256)
                high = pl.ds(pl.multiple_of(half_width + i * 256, 256), 256)
                block = gkv[2 * c : 2 * c + 2, :, :, :, lanes].reshape(256, 256)
                block = dot(perm[...], block).astype(BF)
                keys[64 * c : 64 * c + 64, lanes] = block[:64]
                values[64 * c : 64 * c + 64, lanes] = block[64:128]
                keys[64 * c : 64 * c + 64, high] = block[128:192]
                values[64 * c : 64 * c + 64, high] = block[192:]
                return carry

            lax.fori_loop(0, half_width // 256, sort_in, 0)

        def heads_of(block, count):
            return [block[:, j * HD : (j + 1) * HD] for j in range(count)]

        def chosen_heads(group, carry):
            lanes = pl.ds(pl.multiple_of(group * (8 * HD), 8 * HD), 8 * HD)
            asked, kept = heads_of(pickedq[:, lanes], 8), heads_of(keys[:, lanes], 8)
            scores = [dot(q, k, NT) for q, k in zip(asked, kept)]
            scores = jnp.concatenate(scores, axis=0) * scaling_factor
            weights = jnp.exp(scores - jnp.max(scores, axis=-1, keepdims=True))
            weights = (weights / jnp.sum(weights, axis=-1, keepdims=True)).astype(BF)
            mixed = [
                dot(weights[2 * CAP * j : 2 * CAP * (j + 1)], v)
                for j, v in enumerate(heads_of(values[:, lanes], 8))
            ]
            mixed = jnp.concatenate(mixed, axis=1)
            attended[:, lanes] = picked[:, lanes].astype(F32) + mixed * has_row
            return carry

        lax.fori_loop(0, heads // 8, chosen_heads, 0)
        picked[...] = attended[...].astype(BF)
        put_capacity()

        def forward(group, carry):
            lanes = pl.ds(pl.multiple_of(group * (4 * HD), 4 * HD), 4 * HD)
            asked, kept = heads_of(queries[:, lanes], 4), heads_of(keys[:, lanes], 4)
            scores = [dot(k, q, NT) * scaling_factor for q, k in zip(asked, kept)]
            weights = [jnp.exp(one - jnp.max(one, axis=0, keepdims=True)) for one in scores]
            weights = [one / jnp.sum(one, axis=0, keepdims=True) for one in weights]
            mixed = [
                dot(one.astype(BF), v, TN)
                for one, v in zip(weights, heads_of(values[:, lanes], 4))
            ]
            mixed = jnp.concatenate(mixed, axis=1)
            resid[:, lanes] = (cur[:, lanes].astype(F32) + mixed).astype(BF)
            for j, one in enumerate(weights):
                probs[group * 4 + j] = one
            return carry

        def backward(group, carry):
            lanes = pl.ds(pl.multiple_of(group * (4 * HD), 4 * HD), 4 * HD)
            weights = [probs[group * 4 + j] for j in range(4)]
            upstream, asked = heads_of(cot[:, lanes], 4), heads_of(queries[:, lanes], 4)
            dweights = [dot(v, g, NT) for v, g in zip(heads_of(values[:, lanes], 4), upstream)]
            inner = [
                jnp.sum(d * one, axis=0, keepdims=True) for d, one in zip(dweights, weights)
            ]
            dscores = [
                one * (d - i) * scaling_factor for one, d, i in zip(weights, dweights, inner)
            ]
            high = [one.astype(BF) for one in dscores]
            low = [(one - h.astype(F32)).astype(BF) for one, h in zip(dscores, high)]
            dk = [
                dot(jnp.concatenate([h, l], axis=1), jnp.concatenate([q, q], axis=0))
                for h, l, q in zip(high, low, asked)
            ]
            dv = [dot(one.astype(BF), g) for one, g in zip(weights, upstream)]
            dkeys[:, lanes] = jnp.concatenate(dk, axis=1).astype(BF)
            dvalues[:, lanes] = jnp.concatenate(dv, axis=1).astype(BF)
            return carry

        def part_of(work, i, of):
            count = heads // 4

            def task():
                lax.fori_loop(count * i // of, count * (i + 1) // of, work, 0)

            return task

        def hand_over():
            pass_on(0, resid, before)
            keep(resid).start()
            loads[1].wait()

        drive(
            [gather(links, halves, gcap, cap_base)],
            [part_of(forward, i, 4) for i in range(4)]
            + [hand_over]
            + [part_of(backward, i, 4) for i in range(4)],
        )

        for c in range(2):

            def sort_out(i, carry, c=c):
                lanes = pl.ds(pl.multiple_of(i * 256, 256), 256)
                high = pl.ds(pl.multiple_of(half_width + i * 256, 256), 256)
                rows = slice(64 * c, 64 * c + 64)
                block = jnp.concatenate(
                    [dkeys[rows, lanes], dvalues[rows, lanes], dkeys[rows, high], dvalues[rows, high]],
                    axis=0,
                )
                block = dot(perm_t[...], block).astype(BF)
                gparts[2 * c : 2 * c + 2, :, :, :, lanes] = block.reshape(
                    2, RING, 2, 2 * CAP, 256
                )
                return carry

            lax.fori_loop(0, half_width // 256, sort_out, 0)

        grad_stream = scatter(
            links, halves, gparts, (gland_a, gland_b, gland_c, gland_d, glast), grad_base
        )
        next(grad_stream)
        expert()
        drive([scatter(links, halves, parts, ret_land, ret_base), grad_stream])
        grad_out[...] = gparts[x, y, z].astype(F32) + glast[...].astype(F32)
        finish(resid)
        keep(resid).wait()
        links.finish()


def place_rows(
    base, before, own_rows, their_rows, own_slot, their_slot, grad, layer_out, arriving, grad_out
):
    upper = pl.program_id(0) >= pl.num_programs(0) // 2
    tokens, lanes = base.shape
    row = lax.broadcasted_iota(jnp.int32, (2 * CAP, tokens), 0) - jnp.where(upper, CAP, 0)
    for slots, rows, kept, target in (
        (own_slot[:1, :], own_rows, base, layer_out),
        (their_slot[:1, :], their_rows, before, arriving),
    ):
        chosen = jnp.where(row < 0, 0.0, (slots == row).astype(F32)).astype(BF)
        has = dot(chosen, jnp.ones((2 * CAP, 128), BF), TN)[:, :1] > 0.5
        for start in range(0, lanes, 256):
            part = slice(start, start + 256)
            moved = dot(chosen, rows[:, part], TN)
            target[:, part] = jnp.where(has, moved, kept[:, part].astype(F32)).astype(BF)
    total = jnp.where(upper, grad[CAP:, :], grad[:CAP, :])
    for r in range(grad_out.shape[0]):
        grad_out[r] = total[2 * r : 2 * r + 2]


def local(
    layer_in, memory, cotangent, norm_gain, attn_gain, expert_in, expert_out, slot_index, gate_prob
):
    sections = lax.axis_size("section")
    tokens, width = layer_in.shape[1:]
    rows = memory.shape[1]
    stash = rows * 2 * RING * RING
    ffw = expert_in.shape[2]
    half = width // 2
    heads = width // HD
    vmem = pl.BlockSpec(memory_space=pltpu.VMEM)
    anywhere = pl.BlockSpec(memory_space=pl.ANY)
    full = (RING, RING, 2, 2 * CAP, half)
    quarter = half // 4
    landing = [
        pltpu.VMEM((2, RING, 2, 2, 2 * CAP, quarter), BF),
        pltpu.VMEM((2, RING, 2, 2, 2 * CAP, 2 * quarter), BF),
        pltpu.VMEM((2, 2, 2, 2 * CAP, quarter), BF),
        pltpu.VMEM((2, 2, 2, 2 * CAP, 2 * quarter), BF),
    ]
    count = 2 * GATHER_KEYS + 2 * SCATTER_KEYS + 3
    base, before, own_rows, their_rows, their_slot, grad = pl.pallas_call(
        lambda *refs: kernel(sections, *refs),
        out_shape=(
            jax.ShapeDtypeStruct((tokens, width), BF),
            jax.ShapeDtypeStruct((tokens, width), BF),
            jax.ShapeDtypeStruct((2 * CAP, half), BF),
            jax.ShapeDtypeStruct((2 * CAP, half), BF),
            jax.ShapeDtypeStruct((8, tokens), jnp.int32),
            jax.ShapeDtypeStruct((2 * CAP, half), F32),
        ),
        in_specs=[vmem, anywhere, anywhere, vmem, vmem, anywhere, anywhere, vmem, vmem],
        out_specs=(anywhere, anywhere, vmem, vmem, vmem, vmem),
        scratch_shapes=[
            pltpu.VMEM((tokens, width), BF),
            pltpu.VMEM((tokens, width), BF),
            pltpu.VMEM((ffw, width), BF),
            pltpu.VMEM((ffw, width), BF),
            pltpu.VMEM((tokens, width), BF),
            pltpu.VMEM((tokens, width), BF),
            pltpu.VMEM(full, BF),
            pltpu.VMEM((stash, width), BF),
            pltpu.VMEM((stash, width), BF),
            pltpu.VMEM(full, BF),
            pltpu.VMEM((heads, stash, tokens), F32),
            pltpu.VMEM(full, BF),
            pltpu.VMEM(full, BF),
            pltpu.VMEM((stash, width), BF),
            pltpu.VMEM((stash, width), BF),
            pltpu.VMEM((2 * CAP, width), BF),
            pltpu.VMEM((2 * CAP, width), BF),
            pltpu.VMEM((2 * CAP, width), F32),
            pltpu.VMEM((256, 256), BF),
            pltpu.VMEM((256, 256), BF),
            pltpu.VMEM((2 * RING * RING, CAP, ffw), F32),
            pltpu.VMEM((2 * RING * RING * CAP, ffw), BF),
            pltpu.VMEM((8, tokens), jnp.int32),
            *landing,
            pltpu.VMEM((2 * CAP, half), BF),
            pltpu.VMEM((2 * CAP, half), BF),
            *landing,
            pltpu.SemaphoreType.DMA((6,)),
            pltpu.SemaphoreType.DMA((count,)),
            pltpu.SemaphoreType.DMA((count,)),
        ],
        compiler_params=pltpu.CompilerParams(
            collective_id=0, has_side_effects=True, vmem_limit_bytes=60 * 1024 * 1024
        ),
    )(
        memory[0],
        layer_in[0],
        cotangent[0],
        norm_gain,
        attn_gain,
        expert_in[0].T,
        expert_out[0],
        slot_index,
        gate_prob,
    )
    steps = 4
    lanes = width // steps
    whole = pl.BlockSpec((tokens, lanes), lambda i: (0, i))
    folded = pl.BlockSpec((2 * CAP, lanes), lambda i: (0, i % 2))
    layer_out, arriving, grad_memory = pl.pallas_call(
        place_rows,
        grid=(steps,),
        out_shape=(
            jax.ShapeDtypeStruct((tokens, width), BF),
            jax.ShapeDtypeStruct((tokens, width), BF),
            jax.ShapeDtypeStruct((rows, 2, width), F32),
        ),
        in_specs=[
            whole,
            whole,
            folded,
            folded,
            pl.BlockSpec((1, tokens), lambda i: (0, 0)),
            pl.BlockSpec((8, tokens), lambda i: (0, 0)),
            folded,
        ],
        out_specs=(whole, whole, pl.BlockSpec((rows, 2, lanes), lambda i: (0, 0, i))),
    )(base, before, own_rows, their_rows, slot_index, their_slot, grad)
    return (layer_out[None], arriving[None], grad_memory[None])


def solution(mesh):
    placed = (
        P("section", "expert", None),
        P("section", "expert", None, None),
        P("section", "expert", None),
        P("section", None),
        P("section", None),
        P("section", None, "expert"),
        P("section", "expert", None),
        P("section", "expert"),
        P("section", "expert"),
    )
    return jax.shard_map(
        local,
        mesh=mesh,
        in_specs=placed,
        out_specs=(
            P("section", "expert", None),
            P("section", "expert", None),
            P("section", "expert", None, None),
        ),
        check_vma=False,
    )
```

```python
import jax
import jax.numpy as jnp
from jax import lax
from jax.experimental import pallas as pl
from jax.experimental.pallas import tpu as pltpu
from jax.sharding import PartitionSpec as P

HD = 128
CAP = 8
RING = 4
MESH = pl.DeviceIdType.MESH
BF = jnp.bfloat16
F32 = jnp.float32
NT = (((1,), (1,)), ((), ()))
TN = (((0,), (0,)), ((), ()))


def dot(a, b, dims=(((1,), (0,)), ((), ()))):
    return lax.dot_general(a, b, dims, preferred_element_type=F32)


class Links:
    def __init__(self, send, recv, section, x, y, z):
        self.send, self.recv = send, recv
        self.section, self.x, self.y, self.z = section, x, y, z
        self.started = []

    def copy(self, key, src, dst, device):
        return pltpu.make_async_remote_copy(
            src_ref=src,
            dst_ref=dst,
            send_sem=self.send.at[key],
            recv_sem=self.recv.at[key],
            device_id=device,
            device_id_type=MESH,
        )

    def put(self, key, src, dst, device):
        copy = self.copy(key, src, dst, device)
        copy.start()
        self.started.append(copy)

    def got(self, key, dst, device):
        self.copy(key, dst, dst, device).wait_recv()

    def finish(self):
        for copy in self.started:
            copy.wait_send()
        self.started = []


GROUP = ((2, 0), (2, 1), (1, 0), (3, 0), (1, 1), (3, 1), (0, 1))


class Half:
    def __init__(self, links, first, lane, width):
        self.links, self.first, self.lane, self.width = links, first, lane, width
        self.u, self.v = (links.x, links.y) if first == "x" else (links.y, links.x)

    def at(self, buf, u, v, low=0, size=None):
        lanes = pl.ds(self.lane + low, self.width if size is None else size)
        if self.first == "x":
            return buf.at[u, v, :, :, lanes]
        return buf.at[v, u, :, :, lanes]

    def one(self, buf, u, v, z, low=0, size=None):
        lanes = pl.ds(self.lane + low, self.width if size is None else size)
        if self.first == "x":
            return buf.at[u, v, z, :, lanes]
        return buf.at[v, u, z, :, lanes]

    def device(self, u, v, z=None):
        x, y = (u, v) if self.first == "x" else (v, u)
        z = self.links.z if z is None else z
        return (self.links.section, x * (RING * 2) + y * 2 + z)


def step(i, by):
    return lax.rem(i + by + RING, RING)


GATHER_KEYS = 78
SCATTER_KEYS = 46
PIECES = 1
TURNS = ((0, 1), (1, -1))


def gather(links, halves, buf, base):
    z = links.z
    keyed = [(half, base + 39 * i) for i, half in enumerate(halves)]

    def source(half, slot):
        if slot == 7:
            return half.u, z
        du, dz = GROUP[slot]
        return step(half.u, -du), (z + dz) % 2

    def spread(half, key, slot):
        u, zz = source(half, slot)
        part = half.one(buf, u, half.v, zz)
        for d, turn in TURNS:
            links.put(key + 7 + slot * 4 + d, part, part, half.device(half.u, step(half.v, turn)))

    def relay(slot):
        for half, key in keyed:
            q = half.width // 2
            u, zz = source(half, slot)
            k = key + 7 + slot * 4
            for d, turn in TURNS:
                left = step(half.v, -turn)
                links.got(k + d, half.one(buf, u, left, zz), half.device(half.u, left))
                part = half.one(buf, u, left, zz, d * q, q)
                links.put(k + 2 + d, part, part, half.device(half.u, step(half.v, turn)))

    for i, (du, dz) in enumerate(GROUP):
        for half, key in keyed:
            part = half.one(buf, half.u, half.v, z)
            links.put(key + i, part, part, half.device(step(half.u, du), half.v, (z + dz) % 2))
    for half, key in keyed:
        spread(half, key, 7)
    yield
    order = (6, 2, 3, 4, 5, 0, 1)
    for n, slot in enumerate(order):
        for half, key in keyed:
            u, zz = source(half, slot)
            links.got(key + slot, half.one(buf, u, half.v, zz), half.device(u, half.v, zz))
            spread(half, key, slot)
        if n == 3:
            relay(7)
            yield
    yield
    for n, slot in enumerate(order):
        relay(slot)
        if n in (3, 6):
            yield
    for slot in (7,) + order:
        for half, key in keyed:
            q = half.width // 2
            u, zz = source(half, slot)
            for d, turn in TURNS:
                links.got(
                    key + 7 + slot * 4 + 2 + d,
                    half.one(buf, u, step(half.v, 2), zz, d * q, q),
                    half.device(half.u, step(half.v, -turn)),
                )


def add_into(target, *others):
    total = target[...].astype(F32)
    for other in others:
        total = total + other[...].astype(F32)
    target[...] = total.astype(target.dtype)


def scatter(links, halves, buf, land, base):
    passing, whole, last = land
    z = links.z
    order = ((0, 2), (1, -1), (2, 1), (3, 0))
    keyed = [(i, half, base + 23 * i) for i, half in enumerate(halves)]
    for slot, by in order:
        for i, half, key in keyed:
            q = half.width // 2
            for d, turn in TURNS:
                links.put(
                    key + slot * 4 + d,
                    half.at(buf, step(half.u, by), step(half.v, 2), d * q, q),
                    passing.at[i, slot, d],
                    half.device(half.u, step(half.v, turn)),
                )
    yield
    for slot, by in order:
        for i, half, key in keyed:
            q = half.width // 2
            for d, turn in TURNS:
                to = step(half.v, turn)
                links.got(
                    key + slot * 4 + d,
                    passing.at[i, slot, d],
                    half.device(half.u, step(half.v, -turn)),
                )
                add_into(half.at(buf, step(half.u, by), to, d * q, q), passing.at[i, slot, d])
                links.put(
                    key + slot * 4 + 2 + d,
                    half.at(buf, step(half.u, by), to),
                    whole.at[i, slot, d],
                    half.device(half.u, to),
                )
        yield
    for slot, by in order:
        for i, half, key in keyed:
            for d, turn in TURNS:
                links.got(
                    key + slot * 4 + 2 + d,
                    whole.at[i, slot, d],
                    half.device(half.u, step(half.v, -turn)),
                )
            add_into(
                half.at(buf, step(half.u, by), half.v),
                whole.at[i, slot, 0],
                whole.at[i, slot, 1],
            )
            for j, (du, dz) in enumerate(GROUP):
                if du == by % RING:
                    u, zz = step(half.u, du), (z + dz) % 2
                    links.put(
                        key + 16 + j,
                        half.one(buf, u, half.v, zz),
                        last.at[i, j],
                        half.device(u, half.v, zz),
                    )
        yield
    for i, half, key in keyed:
        for j, (du, dz) in enumerate(GROUP):
            u, zz = step(half.u, -du), (z + dz) % 2
            links.got(key + 16 + j, last.at[i, j], half.device(u, half.v, zz))


def scattered(buf, place, land):
    last = land[2]
    total = buf[place].astype(F32)
    others = [jnp.sum(last[i].astype(F32), axis=0) for i in range(2)]
    return total + jnp.concatenate(others, axis=1)


def drive(streams, tasks=()):
    streams, tasks = list(streams), list(tasks)
    while streams or tasks:
        for stream in list(streams):
            if next(stream, "end") == "end":
                streams.remove(stream)
        if tasks:
            tasks.pop(0)()


def scaled(rows, gain):
    return rows * lax.rsqrt(jnp.mean(rows * rows, axis=-1, keepdims=True) + 1e-06) * gain


def kernel(
    sections,
    mem_ref,
    layer_ref,
    cot_ref,
    norm_ref,
    attn_ref,
    in_ref,
    out_ref,
    slot_ref,
    gate_ref,
    base_out,
    before,
    own_rows,
    their_rows,
    their_slot,
    grad_out,
    cur,
    cot,
    win,
    wout,
    queries,
    resid,
    gkv,
    keys,
    values,
    gcap,
    probs,
    parts,
    gparts,
    dkeys,
    dvalues,
    picked,
    pickedq,
    attended,
    perm,
    perm_t,
    hacc,
    hidden,
    own_slot,
    land_a,
    land_b,
    land_c,
    gland_a,
    gland_b,
    gland_c,
    load_sem,
    send_sem,
    recv_sem,
):
    tokens, width = cur.shape
    half_width = width // 2
    heads = width // HD
    ffw = win.shape[0]
    scaling_factor = HD ** (-0.5)
    section = lax.axis_index("section")
    place = lax.axis_index("expert")
    x, y, z = place // (RING * 2), (place // 2) % RING, place % 2
    links = Links(send_sem, recv_sem, section, x, y, z)
    halves = (
        Half(links, "x", 0, half_width // 2),
        Half(links, "y", half_width // 2, half_width // 2),
    )
    cap_base, kv_base = 0, GATHER_KEYS
    ret_base = kv_base + GATHER_KEYS
    grad_base = ret_base + SCATTER_KEYS
    pass_base = grad_base + SCATTER_KEYS

    loads = [
        pltpu.make_async_copy(src, dst, load_sem.at[i])
        for i, (src, dst) in enumerate(
            ((layer_ref, cur), (cot_ref, cot), (in_ref, win), (out_ref, wout))
        )
    ]
    for load in loads:
        load.start()

    def device(xx, yy, zz):
        return (section, xx * (RING * 2) + yy * 2 + zz)

    barrier = pltpu.get_barrier_semaphore()
    peers = [device(step(x, dx), y, (z + dz) % 2) for dx in range(RING) for dz in range(2) if dx or dz]
    peers += [device(x, step(y, dy), (z + dz) % 2) for dy in range(1, RING) for dz in range(2)]
    for peer in peers:
        pl.semaphore_signal(barrier, inc=1, device_id=peer, device_id_type=MESH)

    @pl.when(section > 0)
    def _():
        pl.semaphore_signal(
            barrier, inc=1, device_id=(section - 1, place), device_id_type=MESH
        )

    @pl.when(section < sections - 1)
    def _():
        pl.semaphore_signal(
            barrier, inc=1, device_id=(section + 1, place), device_id_type=MESH
        )

    ends = jnp.where(section > 0, 1, 0) + jnp.where(section < sections - 1, 1, 0)
    pl.semaphore_wait(barrier, len(peers) + ends)

    def pass_copy(key, src, dst):
        return links.copy(pass_base + key, src, dst, (section + 1, place))

    def pass_on(key, src, dst):
        @pl.when(section < sections - 1)
        def _():
            pass_copy(key, src, dst).start()

    def pass_sent(key, src, dst):
        @pl.when(section < sections - 1)
        def _():
            pass_copy(key, src, dst).wait_send()

    def pass_got(key, dst):
        @pl.when(section > 0)
        def _():
            links.copy(pass_base + key, dst, dst, (section - 1, place)).wait_recv()

    def piece(ref, i):
        return ref.at[:, pl.ds(i * (width // PIECES), width // PIECES)]

    def pass_piece(base, i):
        return lambda: pass_on(2 + i, piece(base, i), piece(before, i))

    slots = slot_ref[...]
    rows16 = lax.broadcasted_iota(jnp.int32, (2 * CAP, tokens), 0)
    onehot = (slots == rows16).astype(F32).astype(BF)
    has_row = jnp.sum((slots == rows16).astype(F32), axis=-1, keepdims=True)

    def pick(source, target):
        def one(i, carry):
            lanes = pl.ds(pl.multiple_of(i * 512, 512), 512)
            target[:, lanes] = dot(onehot, source[:, lanes]).astype(target.dtype)
            return carry

        lax.fori_loop(0, width // 512, one, 0)

    def fold(rows):
        return jnp.concatenate([rows[:CAP, :half_width], rows[:CAP, half_width:]], axis=0)

    def put_capacity():
        rows = picked[...].astype(F32)
        gcap[x, y, z] = fold(scaled(rows, norm_ref[...])).astype(BF)

    def expert():
        loads[2].wait()
        loads[3].wait()
        hacc[...] = jnp.zeros_like(hacc)

        def into(k, carry):
            lanes = pl.ds(pl.multiple_of(k * 256, 256), 256)
            block = gcap[:, :, :, :, lanes].reshape(-1, 256)
            high_lanes = pl.ds(pl.multiple_of(half_width + k * 256, 256), 256)
            low = dot(block, win[:, lanes], NT)
            high = dot(block, win[:, high_lanes], NT)
            low = low.reshape(-1, 2 * CAP, ffw)[:, :CAP]
            high = high.reshape(-1, 2 * CAP, ffw)[:, CAP:]
            hacc[...] += low + high
            return carry

        lax.fori_loop(0, half_width // 256, into, 0)
        hidden[...] = jax.nn.gelu(hacc[...].reshape(-1, ffw)).astype(BF)

        def out(k, carry):
            lanes = pl.ds(pl.multiple_of(k * 256, 256), 256)
            high_lanes = pl.ds(pl.multiple_of(half_width + k * 256, 256), 256)
            low = dot(hidden[...], wout[:, lanes]).reshape(-1, CAP, 256)
            high = dot(hidden[...], wout[:, high_lanes]).reshape(-1, CAP, 256)
            block = jnp.concatenate([low, high], axis=1).astype(BF)
            parts[:, :, :, :, lanes] = block.reshape(RING, RING, 2, 2 * CAP, 256)
            return carry

        lax.fori_loop(0, half_width // 256, out, 0)

    ret_land = (land_a, land_b, land_c)
    grad_land = (gland_a, gland_b, gland_c)

    def finish(base):
        returned = scattered(parts, (x, y, z), ret_land)
        gates = jnp.sum(
            jnp.where(slots == rows16[:CAP], gate_ref[...], 0.0), axis=-1, keepdims=True
        )
        gates = jnp.concatenate([gates, gates], axis=0)
        own_rows[...] = (fold(picked[...].astype(F32)) + gates * returned).astype(BF)
        pass_on(0, own_rows, their_rows)
        for i in range(PIECES):
            pass_got(2 + i, piece(before, i))
        pass_got(1, their_slot)
        pass_got(0, their_rows)

        for i in range(PIECES):
            pass_sent(2 + i, piece(base, i), piece(before, i))
        pass_sent(1, own_slot, their_slot)
        pass_sent(0, own_rows, their_rows)

    own_slot[...] = jnp.broadcast_to(slots, own_slot.shape)
    nothing = pltpu.make_async_copy(resid, before, load_sem.at[5])

    def keep(base):
        return pltpu.make_async_copy(base, base_out, load_sem.at[4])

    @pl.when(section < sections // 2)
    def _():
        loads[0].wait()
        pick(cur, picked)
        put_capacity()
        stream = gather(links, halves, gcap, cap_base)
        next(stream)
        pass_on(1, own_slot, their_slot)
        keep(cur).start()

        @pl.when(section == 0)
        def _():
            resid[...] = jnp.zeros_like(resid)
            nothing.start()
            their_slot[...] = jnp.full_like(their_slot, -1)
            their_rows[...] = jnp.zeros_like(their_rows)

        drive([stream])
        loads[1].wait()
        expert()
        pass_piece(cur, 0)()
        drive([scatter(links, halves, parts, ret_land, ret_base)])
        grad_out[...] = jnp.zeros_like(grad_out)
        finish(cur)
        keep(cur).wait()

        @pl.when(section == 0)
        def _():
            nothing.wait()

        links.finish()

    @pl.when(section >= sections // 2)
    def _():
        rows = [mem_ref[r].astype(F32) for r in range(mem_ref.shape[0])]
        gkv[x, y, z] = fold(jnp.concatenate(rows, axis=0)).astype(BF)

        def make_perm():
            for target, flip in ((perm, 0), (perm_t, 1)):
                k = lax.broadcasted_iota(jnp.int32, (256, 256), flip)
                i = lax.broadcasted_iota(jnp.int32, (256, 256), 1 - flip)
                m = k & 63
                source = ((m >> 2) << 4) + ((k >> 7) << 3) + ((m & 3) << 1) + ((k >> 6) & 1)
                target[...] = (source == i).astype(F32).astype(BF)

        def make_queries():
            loads[0].wait()

            def one(i, carry):
                rows = pl.ds(pl.multiple_of(i * 16, 16), 16)
                queries[rows, :] = scaled(cur[rows, :].astype(F32), attn_ref[...]).astype(BF)
                return carry

            lax.fori_loop(0, tokens // 16, one, 0)

        def pick_rows():
            pick(cur, picked)
            pick(queries, pickedq)

        drive(
            [gather(links, halves, gkv, kv_base)],
            [lambda: pass_on(1, own_slot, their_slot), make_perm, make_queries, pick_rows],
        )

        for c in range(2):

            def sort_in(i, carry, c=c):
                lanes = pl.ds(pl.multiple_of(i * 256, 256), 256)
                high = pl.ds(pl.multiple_of(half_width + i * 256, 256), 256)
                block = gkv[2 * c : 2 * c + 2, :, :, :, lanes].reshape(256, 256)
                block = dot(perm[...], block).astype(BF)
                keys[64 * c : 64 * c + 64, lanes] = block[:64]
                values[64 * c : 64 * c + 64, lanes] = block[64:128]
                keys[64 * c : 64 * c + 64, high] = block[128:192]
                values[64 * c : 64 * c + 64, high] = block[192:]
                return carry

            lax.fori_loop(0, half_width // 256, sort_in, 0)

        def heads_of(block, count):
            return [block[:, j * HD : (j + 1) * HD] for j in range(count)]

        def chosen_heads(group, carry):
            lanes = pl.ds(pl.multiple_of(group * (8 * HD), 8 * HD), 8 * HD)
            asked, kept = heads_of(pickedq[:, lanes], 8), heads_of(keys[:, lanes], 8)
            scores = [dot(q, k, NT) for q, k in zip(asked, kept)]
            scores = jnp.concatenate(scores, axis=0) * scaling_factor
            weights = jnp.exp(scores - jnp.max(scores, axis=-1, keepdims=True))
            weights = (weights / jnp.sum(weights, axis=-1, keepdims=True)).astype(BF)
            mixed = [
                dot(weights[2 * CAP * j : 2 * CAP * (j + 1)], v)
                for j, v in enumerate(heads_of(values[:, lanes], 8))
            ]
            mixed = jnp.concatenate(mixed, axis=1)
            attended[:, lanes] = picked[:, lanes].astype(F32) + mixed * has_row
            return carry

        lax.fori_loop(0, heads // 8, chosen_heads, 0)
        picked[...] = attended[...].astype(BF)
        put_capacity()

        def forward(group, carry):
            lanes = pl.ds(pl.multiple_of(group * (4 * HD), 4 * HD), 4 * HD)
            asked, kept = heads_of(queries[:, lanes], 4), heads_of(keys[:, lanes], 4)
            scores = [dot(k, q, NT) * scaling_factor for q, k in zip(asked, kept)]
            weights = [jnp.exp(one - jnp.max(one, axis=0, keepdims=True)) for one in scores]
            weights = [one / jnp.sum(one, axis=0, keepdims=True) for one in weights]
            mixed = [
                dot(one.astype(BF), v, TN)
                for one, v in zip(weights, heads_of(values[:, lanes], 4))
            ]
            mixed = jnp.concatenate(mixed, axis=1)
            resid[:, lanes] = (cur[:, lanes].astype(F32) + mixed).astype(BF)
            for j, one in enumerate(weights):
                probs[group * 4 + j] = one
            return carry

        def backward(group, carry):
            lanes = pl.ds(pl.multiple_of(group * (4 * HD), 4 * HD), 4 * HD)
            weights = [probs[group * 4 + j] for j in range(4)]
            upstream, asked = heads_of(cot[:, lanes], 4), heads_of(queries[:, lanes], 4)
            dweights = [dot(v, g, NT) for v, g in zip(heads_of(values[:, lanes], 4), upstream)]
            inner = [
                jnp.sum(d * one, axis=0, keepdims=True) for d, one in zip(dweights, weights)
            ]
            dscores = [
                one * (d - i) * scaling_factor for one, d, i in zip(weights, dweights, inner)
            ]
            high = [one.astype(BF) for one in dscores]
            low = [(one - h.astype(F32)).astype(BF) for one, h in zip(dscores, high)]
            dk = [
                dot(jnp.concatenate([h, l], axis=1), jnp.concatenate([q, q], axis=0))
                for h, l, q in zip(high, low, asked)
            ]
            dv = [dot(one.astype(BF), g) for one, g in zip(weights, upstream)]
            dkeys[:, lanes] = jnp.concatenate(dk, axis=1).astype(BF)
            dvalues[:, lanes] = jnp.concatenate(dv, axis=1).astype(BF)
            return carry

        def part_of(work, i, of):
            count = heads // 4

            def task():
                lax.fori_loop(count * i // of, count * (i + 1) // of, work, 0)

            return task

        def forward_piece(i):
            def task():
                of = heads // 4 // PIECES
                lax.fori_loop(i * of, (i + 1) * of, forward, 0)
                pass_piece(resid, i)()

            return task

        def keep_rows():
            keep(resid).start()
            loads[1].wait()

        drive(
            [gather(links, halves, gcap, cap_base)],
            [forward_piece(i) for i in range(PIECES)]
            + [keep_rows]
            + [part_of(backward, i, 4) for i in range(4)],
        )

        for c in range(2):

            def sort_out(i, carry, c=c):
                lanes = pl.ds(pl.multiple_of(i * 256, 256), 256)
                high = pl.ds(pl.multiple_of(half_width + i * 256, 256), 256)
                rows = slice(64 * c, 64 * c + 64)
                block = jnp.concatenate(
                    [dkeys[rows, lanes], dvalues[rows, lanes], dkeys[rows, high], dvalues[rows, high]],
                    axis=0,
                )
                block = dot(perm_t[...], block).astype(BF)
                gparts[2 * c : 2 * c + 2, :, :, :, lanes] = block.reshape(
                    2, RING, 2, 2 * CAP, 256
                )
                return carry

            lax.fori_loop(0, half_width // 256, sort_out, 0)

        grad_stream = scatter(
            links, halves, gparts, grad_land, grad_base
        )
        next(grad_stream)
        expert()
        drive([scatter(links, halves, parts, ret_land, ret_base), grad_stream])
        grad_out[...] = scattered(gparts, (x, y, z), grad_land)
        finish(resid)
        keep(resid).wait()
        links.finish()


def place_rows(
    base, before, own_rows, their_rows, own_slot, their_slot, grad, layer_out, arriving, grad_out
):
    upper = pl.program_id(0) >= pl.num_programs(0) // 2
    tokens, lanes = base.shape
    row = lax.broadcasted_iota(jnp.int32, (2 * CAP, tokens), 0) - jnp.where(upper, CAP, 0)
    for slots, rows, kept, target in (
        (own_slot[:1, :], own_rows, base, layer_out),
        (their_slot[:1, :], their_rows, before, arriving),
    ):
        chosen = jnp.where(row < 0, 0.0, (slots == row).astype(F32)).astype(BF)
        has = dot(chosen, jnp.ones((2 * CAP, 128), BF), TN)[:, :1] > 0.5
        for start in range(0, lanes, 256):
            part = slice(start, start + 256)
            moved = dot(chosen, rows[:, part], TN)
            target[:, part] = jnp.where(has, moved, kept[:, part].astype(F32)).astype(BF)
    total = jnp.where(upper, grad[CAP:, :], grad[:CAP, :])
    for r in range(grad_out.shape[0]):
        grad_out[r] = total[2 * r : 2 * r + 2]


def local(
    layer_in, memory, cotangent, norm_gain, attn_gain, expert_in, expert_out, slot_index, gate_prob
):
    sections = lax.axis_size("section")
    tokens, width = layer_in.shape[1:]
    rows = memory.shape[1]
    stash = rows * 2 * RING * RING
    ffw = expert_in.shape[2]
    half = width // 2
    heads = width // HD
    vmem = pl.BlockSpec(memory_space=pltpu.VMEM)
    anywhere = pl.BlockSpec(memory_space=pl.ANY)
    full = (RING, RING, 2, 2 * CAP, half)
    quarter = half // 4
    landing = [
        pltpu.VMEM((2, RING, 2, 2, 2 * CAP, quarter), BF),
        pltpu.VMEM((2, RING, 2, 2, 2 * CAP, 2 * quarter), BF),
        pltpu.VMEM((2, len(GROUP), 2 * CAP, 2 * quarter), BF),
    ]
    count = 2 * GATHER_KEYS + 2 * SCATTER_KEYS + PIECES + 2
    base, before, own_rows, their_rows, their_slot, grad = pl.pallas_call(
        lambda *refs: kernel(sections, *refs),
        out_shape=(
            jax.ShapeDtypeStruct((tokens, width), BF),
            jax.ShapeDtypeStruct((tokens, width), BF),
            jax.ShapeDtypeStruct((2 * CAP, half), BF),
            jax.ShapeDtypeStruct((2 * CAP, half), BF),
            jax.ShapeDtypeStruct((8, tokens), jnp.int32),
            jax.ShapeDtypeStruct((2 * CAP, half), F32),
        ),
        in_specs=[vmem, anywhere, anywhere, vmem, vmem, anywhere, anywhere, vmem, vmem],
        out_specs=(anywhere, anywhere, vmem, vmem, vmem, vmem),
        scratch_shapes=[
            pltpu.VMEM((tokens, width), BF),
            pltpu.VMEM((tokens, width), BF),
            pltpu.VMEM((ffw, width), BF),
            pltpu.VMEM((ffw, width), BF),
            pltpu.VMEM((tokens, width), BF),
            pltpu.VMEM((tokens, width), BF),
            pltpu.VMEM(full, BF),
            pltpu.VMEM((stash, width), BF),
            pltpu.VMEM((stash, width), BF),
            pltpu.VMEM(full, BF),
            pltpu.VMEM((heads, stash, tokens), F32),
            pltpu.VMEM(full, BF),
            pltpu.VMEM(full, BF),
            pltpu.VMEM((stash, width), BF),
            pltpu.VMEM((stash, width), BF),
            pltpu.VMEM((2 * CAP, width), BF),
            pltpu.VMEM((2 * CAP, width), BF),
            pltpu.VMEM((2 * CAP, width), F32),
            pltpu.VMEM((256, 256), BF),
            pltpu.VMEM((256, 256), BF),
            pltpu.VMEM((2 * RING * RING, CAP, ffw), F32),
            pltpu.VMEM((2 * RING * RING * CAP, ffw), BF),
            pltpu.VMEM((8, tokens), jnp.int32),
            *landing,
            *landing,
            pltpu.SemaphoreType.DMA((6,)),
            pltpu.SemaphoreType.DMA((count,)),
            pltpu.SemaphoreType.DMA((count,)),
        ],
        compiler_params=pltpu.CompilerParams(
            collective_id=0, has_side_effects=True, vmem_limit_bytes=60 * 1024 * 1024
        ),
    )(
        memory[0],
        layer_in[0],
        cotangent[0],
        norm_gain,
        attn_gain,
        expert_in[0].T,
        expert_out[0],
        slot_index,
        gate_prob,
    )
    steps = 4
    lanes = width // steps
    whole = pl.BlockSpec((tokens, lanes), lambda i: (0, i))
    folded = pl.BlockSpec((2 * CAP, lanes), lambda i: (0, i % 2))
    layer_out, arriving, grad_memory = pl.pallas_call(
        place_rows,
        grid=(steps,),
        out_shape=(
            jax.ShapeDtypeStruct((tokens, width), BF),
            jax.ShapeDtypeStruct((tokens, width), BF),
            jax.ShapeDtypeStruct((rows, 2, width), F32),
        ),
        in_specs=[
            whole,
            whole,
            folded,
            folded,
            pl.BlockSpec((1, tokens), lambda i: (0, 0)),
            pl.BlockSpec((8, tokens), lambda i: (0, 0)),
            folded,
        ],
        out_specs=(whole, whole, pl.BlockSpec((rows, 2, lanes), lambda i: (0, 0, i))),
    )(base, before, own_rows, their_rows, slot_index, their_slot, grad)
    return (layer_out[None], arriving[None], grad_memory[None])


def solution(mesh):
    placed = (
        P("section", "expert", None),
        P("section", "expert", None, None),
        P("section", "expert", None),
        P("section", None),
        P("section", None),
        P("section", None, "expert"),
        P("section", "expert", None),
        P("section", "expert"),
        P("section", "expert"),
    )
    return jax.shard_map(
        local,
        mesh=mesh,
        in_specs=placed,
        out_specs=(
            P("section", "expert", None),
            P("section", "expert", None),
            P("section", "expert", None, None),
        ),
        check_vma=False,
    )
```

```python
import jax
import jax.numpy as jnp
from jax import lax
from jax.experimental import pallas as pl
from jax.experimental.pallas import tpu as pltpu
from jax.sharding import PartitionSpec as P

HD = 128
CAP = 8
RING = 4
MESH = pl.DeviceIdType.MESH
BF = jnp.bfloat16
F32 = jnp.float32
NT = (((1,), (1,)), ((), ()))
TN = (((0,), (0,)), ((), ()))


def dot(a, b, dims=(((1,), (0,)), ((), ()))):
    return lax.dot_general(a, b, dims, preferred_element_type=F32)


class Links:
    def __init__(self, send, recv, section, x, y, z):
        self.send, self.recv = send, recv
        self.section, self.x, self.y, self.z = section, x, y, z
        self.started = []

    def copy(self, key, src, dst, device):
        return pltpu.make_async_remote_copy(
            src_ref=src,
            dst_ref=dst,
            send_sem=self.send.at[key],
            recv_sem=self.recv.at[key],
            device_id=device,
            device_id_type=MESH,
        )

    def put(self, key, src, dst, device):
        copy = self.copy(key, src, dst, device)
        copy.start()
        self.started.append(copy)

    def got(self, key, dst, device):
        self.copy(key, dst, dst, device).wait_recv()

    def finish(self):
        for copy in self.started:
            copy.wait_send()
        self.started = []


GROUP = ((2, 0), (2, 1), (1, 0), (3, 0), (1, 1), (3, 1), (0, 1))


class Half:
    def __init__(self, links, first, lane, width):
        self.links, self.first, self.lane, self.width = links, first, lane, width
        self.u, self.v = (links.x, links.y) if first == "x" else (links.y, links.x)

    def at(self, buf, u, v, low=0, size=None):
        lanes = pl.ds(self.lane + low, self.width if size is None else size)
        if self.first == "x":
            return buf.at[u, v, :, :, lanes]
        return buf.at[v, u, :, :, lanes]

    def one(self, buf, u, v, z, low=0, size=None):
        lanes = pl.ds(self.lane + low, self.width if size is None else size)
        if self.first == "x":
            return buf.at[u, v, z, :, lanes]
        return buf.at[v, u, z, :, lanes]

    def device(self, u, v, z=None):
        x, y = (u, v) if self.first == "x" else (v, u)
        z = self.links.z if z is None else z
        return (self.links.section, x * (RING * 2) + y * 2 + z)


def step(i, by):
    return lax.rem(i + by + RING, RING)


GATHER_KEYS = 78
SCATTER_KEYS = 46
PIECES = 1
TURNS = ((0, 1), (1, -1))


def gather(links, halves, buf, base):
    z = links.z
    keyed = [(half, base + 39 * i) for i, half in enumerate(halves)]

    def source(half, slot):
        if slot == 7:
            return half.u, z
        du, dz = GROUP[slot]
        return step(half.u, -du), (z + dz) % 2

    def spread(half, key, slot):
        u, zz = source(half, slot)
        part = half.one(buf, u, half.v, zz)
        for d, turn in TURNS:
            links.put(key + 7 + slot * 4 + d, part, part, half.device(half.u, step(half.v, turn)))

    def relay(slot):
        for half, key in keyed:
            q = half.width // 2
            u, zz = source(half, slot)
            k = key + 7 + slot * 4
            for d, turn in TURNS:
                left = step(half.v, -turn)
                links.got(k + d, half.one(buf, u, left, zz), half.device(half.u, left))
                part = half.one(buf, u, left, zz, d * q, q)
                links.put(k + 2 + d, part, part, half.device(half.u, step(half.v, turn)))

    for i, (du, dz) in enumerate(GROUP):
        for half, key in keyed:
            part = half.one(buf, half.u, half.v, z)
            links.put(key + i, part, part, half.device(step(half.u, du), half.v, (z + dz) % 2))
    for half, key in keyed:
        spread(half, key, 7)
    yield
    order = (6, 2, 3, 4, 5, 0, 1)
    for n, slot in enumerate(order):
        for half, key in keyed:
            u, zz = source(half, slot)
            links.got(key + slot, half.one(buf, u, half.v, zz), half.device(u, half.v, zz))
            spread(half, key, slot)
        if n == 3:
            relay(7)
            yield
    yield
    for n, slot in enumerate(order):
        relay(slot)
        if n in (3, 6):
            yield
    for slot in (7,) + order:
        for half, key in keyed:
            q = half.width // 2
            u, zz = source(half, slot)
            for d, turn in TURNS:
                links.got(
                    key + 7 + slot * 4 + 2 + d,
                    half.one(buf, u, step(half.v, 2), zz, d * q, q),
                    half.device(half.u, step(half.v, -turn)),
                )


def add_into(target, *others):
    total = target[...].astype(F32)
    for other in others:
        total = total + other[...].astype(F32)
    target[...] = total.astype(target.dtype)


def scatter(links, halves, buf, land, base):
    passing, whole, last = land
    z = links.z
    order = ((0, 2), (1, -1), (2, 1), (3, 0))
    keyed = [(i, half, base + 23 * i) for i, half in enumerate(halves)]
    for slot, by in order:
        for i, half, key in keyed:
            q = half.width // 2
            for d, turn in TURNS:
                links.put(
                    key + slot * 4 + d,
                    half.at(buf, step(half.u, by), step(half.v, 2), d * q, q),
                    passing.at[i, slot, d],
                    half.device(half.u, step(half.v, turn)),
                )
    yield
    for slot, by in order:
        for i, half, key in keyed:
            q = half.width // 2
            for d, turn in TURNS:
                to = step(half.v, turn)
                links.got(
                    key + slot * 4 + d,
                    passing.at[i, slot, d],
                    half.device(half.u, step(half.v, -turn)),
                )
                add_into(half.at(buf, step(half.u, by), to, d * q, q), passing.at[i, slot, d])
                links.put(
                    key + slot * 4 + 2 + d,
                    half.at(buf, step(half.u, by), to),
                    whole.at[i, slot, d],
                    half.device(half.u, to),
                )
        yield
    for slot, by in order:
        for i, half, key in keyed:
            for d, turn in TURNS:
                links.got(
                    key + slot * 4 + 2 + d,
                    whole.at[i, slot, d],
                    half.device(half.u, step(half.v, -turn)),
                )
            add_into(
                half.at(buf, step(half.u, by), half.v),
                whole.at[i, slot, 0],
                whole.at[i, slot, 1],
            )
            for j, (du, dz) in enumerate(GROUP):
                if du == by % RING:
                    u, zz = step(half.u, du), (z + dz) % 2
                    links.put(
                        key + 16 + j,
                        half.one(buf, u, half.v, zz),
                        last.at[i, j],
                        half.device(u, half.v, zz),
                    )
        yield
    for i, half, key in keyed:
        for j, (du, dz) in enumerate(GROUP):
            u, zz = step(half.u, -du), (z + dz) % 2
            links.got(key + 16 + j, last.at[i, j], half.device(u, half.v, zz))


def scattered(buf, place, land):
    last = land[2]
    total = buf[place].astype(F32)
    others = [jnp.sum(last[i].astype(F32), axis=0) for i in range(2)]
    return total + jnp.concatenate(others, axis=1)


def drive(streams, tasks=()):
    streams, tasks = list(streams), list(tasks)
    while streams or tasks:
        for stream in list(streams):
            if next(stream, "end") == "end":
                streams.remove(stream)
        if tasks:
            tasks.pop(0)()


def scaled(rows, gain):
    return rows * lax.rsqrt(jnp.mean(rows * rows, axis=-1, keepdims=True) + 1e-06) * gain


def kernel(
    sections,
    mem_ref,
    layer_ref,
    cot_ref,
    norm_ref,
    attn_ref,
    in_ref,
    out_ref,
    slot_ref,
    gate_ref,
    base_out,
    before,
    own_rows,
    their_rows,
    their_slot,
    grad_out,
    cur,
    cot,
    win,
    wout,
    queries,
    resid,
    gkv,
    keys,
    values,
    gcap,
    probs,
    parts,
    gparts,
    dkeys,
    dvalues,
    picked,
    pickedq,
    attended,
    perm,
    perm_t,
    hacc,
    hidden,
    own_slot,
    land_a,
    land_b,
    land_c,
    gland_a,
    gland_b,
    gland_c,
    load_sem,
    send_sem,
    recv_sem,
):
    tokens, width = cur.shape
    half_width = width // 2
    heads = width // HD
    ffw = win.shape[0]
    scaling_factor = HD ** (-0.5)
    section = lax.axis_index("section")
    place = lax.axis_index("expert")
    x, y, z = place // (RING * 2), (place // 2) % RING, place % 2
    links = Links(send_sem, recv_sem, section, x, y, z)
    halves = (
        Half(links, "x", 0, half_width // 2),
        Half(links, "y", half_width // 2, half_width // 2),
    )
    cap_base, kv_base = 0, GATHER_KEYS
    ret_base = kv_base + GATHER_KEYS
    grad_base = ret_base + SCATTER_KEYS
    pass_base = grad_base + SCATTER_KEYS

    loads = [
        pltpu.make_async_copy(src, dst, load_sem.at[i])
        for i, (src, dst) in enumerate(
            ((layer_ref, cur), (cot_ref, cot), (in_ref, win), (out_ref, wout))
        )
    ]
    for load in loads:
        load.start()

    def device(xx, yy, zz):
        return (section, xx * (RING * 2) + yy * 2 + zz)

    barrier = pltpu.get_barrier_semaphore()
    peers = [device(step(x, dx), y, (z + dz) % 2) for dx in range(RING) for dz in range(2) if dx or dz]
    peers += [device(x, step(y, dy), (z + dz) % 2) for dy in range(1, RING) for dz in range(2)]
    for peer in peers:
        pl.semaphore_signal(barrier, inc=1, device_id=peer, device_id_type=MESH)

    @pl.when(section > 0)
    def _():
        pl.semaphore_signal(
            barrier, inc=1, device_id=(section - 1, place), device_id_type=MESH
        )

    @pl.when(section < sections - 1)
    def _():
        pl.semaphore_signal(
            barrier, inc=1, device_id=(section + 1, place), device_id_type=MESH
        )

    ends = jnp.where(section > 0, 1, 0) + jnp.where(section < sections - 1, 1, 0)
    pl.semaphore_wait(barrier, len(peers) + ends)

    def pass_copy(key, src, dst):
        return links.copy(pass_base + key, src, dst, (section + 1, place))

    def pass_on(key, src, dst):
        @pl.when(section < sections - 1)
        def _():
            pass_copy(key, src, dst).start()

    def pass_sent(key, src, dst):
        @pl.when(section < sections - 1)
        def _():
            pass_copy(key, src, dst).wait_send()

    def pass_got(key, dst):
        @pl.when(section > 0)
        def _():
            links.copy(pass_base + key, dst, dst, (section - 1, place)).wait_recv()

    def piece(ref, i):
        return ref.at[:, pl.ds(i * (width // PIECES), width // PIECES)]

    def pass_piece(base, i):
        return lambda: pass_on(2 + i, piece(base, i), piece(before, i))

    slots = slot_ref[...]
    rows16 = lax.broadcasted_iota(jnp.int32, (2 * CAP, tokens), 0)
    onehot = (slots == rows16).astype(F32).astype(BF)
    has_row = jnp.sum((slots == rows16).astype(F32), axis=-1, keepdims=True)

    def pick(source, target):
        def one(i, carry):
            lanes = pl.ds(pl.multiple_of(i * 512, 512), 512)
            target[:, lanes] = dot(onehot, source[:, lanes]).astype(target.dtype)
            return carry

        lax.fori_loop(0, width // 512, one, 0)

    def fold(rows):
        return jnp.concatenate([rows[:CAP, :half_width], rows[:CAP, half_width:]], axis=0)

    def put_capacity():
        rows = picked[...].astype(F32)
        gcap[x, y, z] = fold(scaled(rows, norm_ref[...])).astype(BF)

    def expert():
        loads[2].wait()
        loads[3].wait()
        hacc[...] = jnp.zeros_like(hacc)

        def into(k, carry):
            lanes = pl.ds(pl.multiple_of(k * 256, 256), 256)
            block = gcap[:, :, :, :, lanes].reshape(-1, 2 * CAP, 256).astype(F32)
            low = block[:, :CAP].reshape(-1, 256).astype(BF)
            high = block[:, CAP:].reshape(-1, 256).astype(BF)
            high_lanes = pl.ds(pl.multiple_of(half_width + k * 256, 256), 256)
            hacc[...] += dot(win[:, lanes], low, NT) + dot(win[:, high_lanes], high, NT)
            return carry

        lax.fori_loop(0, half_width // 256, into, 0)
        hidden[...] = jax.nn.gelu(hacc[...]).T.astype(BF)

        def out(k, carry):
            lanes = pl.ds(pl.multiple_of(k * 256, 256), 256)
            high_lanes = pl.ds(pl.multiple_of(half_width + k * 256, 256), 256)
            low = dot(hidden[...], wout[:, lanes]).reshape(-1, CAP, 256)
            high = dot(hidden[...], wout[:, high_lanes]).reshape(-1, CAP, 256)
            block = jnp.concatenate([low, high], axis=1).astype(BF)
            parts[:, :, :, :, lanes] = block.reshape(RING, RING, 2, 2 * CAP, 256)
            return carry

        lax.fori_loop(0, half_width // 256, out, 0)

    ret_land = (land_a, land_b, land_c)
    grad_land = (gland_a, gland_b, gland_c)

    def finish(base):
        returned = scattered(parts, (x, y, z), ret_land)
        gates = jnp.sum(
            jnp.where(slots == rows16[:CAP], gate_ref[...], 0.0), axis=-1, keepdims=True
        )
        gates = jnp.concatenate([gates, gates], axis=0)
        own_rows[...] = (fold(picked[...].astype(F32)) + gates * returned).astype(BF)
        pass_on(0, own_rows, their_rows)
        for i in range(PIECES):
            pass_got(2 + i, piece(before, i))
        pass_got(1, their_slot)
        pass_got(0, their_rows)

        for i in range(PIECES):
            pass_sent(2 + i, piece(base, i), piece(before, i))
        pass_sent(1, own_slot, their_slot)
        pass_sent(0, own_rows, their_rows)

    own_slot[...] = jnp.broadcast_to(slots, own_slot.shape)
    nothing = pltpu.make_async_copy(resid, before, load_sem.at[5])

    def keep(base):
        return pltpu.make_async_copy(base, base_out, load_sem.at[4])

    @pl.when(section < sections // 2)
    def _():
        loads[0].wait()
        pick(cur, picked)
        put_capacity()
        stream = gather(links, halves, gcap, cap_base)
        next(stream)
        pass_on(1, own_slot, their_slot)
        keep(cur).start()

        @pl.when(section == 0)
        def _():
            resid[...] = jnp.zeros_like(resid)
            nothing.start()
            their_slot[...] = jnp.full_like(their_slot, -1)
            their_rows[...] = jnp.zeros_like(their_rows)

        drive([stream])
        loads[1].wait()
        expert()
        pass_piece(cur, 0)()
        drive([scatter(links, halves, parts, ret_land, ret_base)])
        grad_out[...] = jnp.zeros_like(grad_out)
        finish(cur)
        keep(cur).wait()

        @pl.when(section == 0)
        def _():
            nothing.wait()

        links.finish()

    @pl.when(section >= sections // 2)
    def _():
        rows = [mem_ref[r].astype(F32) for r in range(mem_ref.shape[0])]
        gkv[x, y, z] = fold(jnp.concatenate(rows, axis=0)).astype(BF)

        def make_perm():
            for target, flip in ((perm, 0), (perm_t, 1)):
                k = lax.broadcasted_iota(jnp.int32, (256, 256), flip)
                i = lax.broadcasted_iota(jnp.int32, (256, 256), 1 - flip)
                m = k & 63
                source = ((m >> 2) << 4) + ((k >> 7) << 3) + ((m & 3) << 1) + ((k >> 6) & 1)
                target[...] = (source == i).astype(F32).astype(BF)

        def make_queries():
            loads[0].wait()

            def one(i, carry):
                rows = pl.ds(pl.multiple_of(i * 16, 16), 16)
                queries[rows, :] = scaled(cur[rows, :].astype(F32), attn_ref[...]).astype(BF)
                return carry

            lax.fori_loop(0, tokens // 16, one, 0)

        def pick_rows():
            pick(cur, picked)
            pick(queries, pickedq)

        drive(
            [gather(links, halves, gkv, kv_base)],
            [lambda: pass_on(1, own_slot, their_slot), make_perm, make_queries, pick_rows],
        )

        def sort_in(i, carry):
            lanes = pl.ds(pl.multiple_of(i * 256, 256), 256)
            high = pl.ds(pl.multiple_of(half_width + i * 256, 256), 256)
            blocks = [gkv[2 * c : 2 * c + 2, :, :, :, lanes].reshape(256, 256) for c in range(2)]
            blocks = [dot(perm[...], block).astype(BF) for block in blocks]
            for start, target, place in (
                (0, keys, lanes),
                (64, values, lanes),
                (128, keys, high),
                (192, values, high),
            ):
                target[:, place] = jnp.concatenate(
                    [block[start : start + 64] for block in blocks], axis=0
                )
            return carry

        lax.fori_loop(0, half_width // 256, sort_in, 0)

        def heads_of(block, count):
            return [block[:, j * HD : (j + 1) * HD] for j in range(count)]

        def chosen_heads(group, carry):
            lanes = pl.ds(pl.multiple_of(group * (20 * HD), 20 * HD), 20 * HD)
            asked, kept = heads_of(pickedq[:, lanes], 20), heads_of(keys[:, lanes], 20)
            scores = [dot(q, k, NT) for q, k in zip(asked, kept)]
            scores = jnp.concatenate(scores, axis=0) * scaling_factor
            weights = jnp.exp(scores - jnp.max(scores, axis=-1, keepdims=True))
            weights = (weights / jnp.sum(weights, axis=-1, keepdims=True)).astype(BF)
            mixed = [
                dot(weights[2 * CAP * j : 2 * CAP * (j + 1)], v)
                for j, v in enumerate(heads_of(values[:, lanes], 20))
            ]
            mixed = jnp.concatenate(mixed, axis=1)
            attended[:, lanes] = picked[:, lanes].astype(F32) + mixed * has_row
            return carry

        lax.fori_loop(0, heads // 20, chosen_heads, 0)
        picked[...] = attended[...].astype(BF)
        put_capacity()

        def forward(group, carry):
            lanes = pl.ds(pl.multiple_of(group * (4 * HD), 4 * HD), 4 * HD)
            asked, kept = heads_of(queries[:, lanes], 4), heads_of(keys[:, lanes], 4)
            scores = [dot(k, q, NT) * scaling_factor for q, k in zip(asked, kept)]
            weights = [jnp.exp(one - jnp.max(one, axis=0, keepdims=True)) for one in scores]
            weights = [one / jnp.sum(one, axis=0, keepdims=True) for one in weights]
            mixed = [
                dot(one.astype(BF), v, TN)
                for one, v in zip(weights, heads_of(values[:, lanes], 4))
            ]
            mixed = jnp.concatenate(mixed, axis=1)
            resid[:, lanes] = (cur[:, lanes].astype(F32) + mixed).astype(BF)
            for j, one in enumerate(weights):
                probs[group * 4 + j] = one
            return carry

        def backward(group, carry):
            lanes = pl.ds(pl.multiple_of(group * (4 * HD), 4 * HD), 4 * HD)
            weights = [probs[group * 4 + j] for j in range(4)]
            upstream, asked = heads_of(cot[:, lanes], 4), heads_of(queries[:, lanes], 4)
            dweights = [dot(v, g, NT) for v, g in zip(heads_of(values[:, lanes], 4), upstream)]
            inner = [
                jnp.sum(d * one, axis=0, keepdims=True) for d, one in zip(dweights, weights)
            ]
            dscores = [
                one * (d - i) * scaling_factor for one, d, i in zip(weights, dweights, inner)
            ]
            high = [one.astype(BF) for one in dscores]
            low = [(one - h.astype(F32)).astype(BF) for one, h in zip(dscores, high)]
            dk = [
                dot(jnp.concatenate([h, l], axis=1), jnp.concatenate([q, q], axis=0))
                for h, l, q in zip(high, low, asked)
            ]
            dv = [dot(one.astype(BF), g) for one, g in zip(weights, upstream)]
            dkeys[:, lanes] = jnp.concatenate(dk, axis=1).astype(BF)
            dvalues[:, lanes] = jnp.concatenate(dv, axis=1).astype(BF)
            return carry

        def part_of(work, i, of):
            count = heads // 4

            def task():
                lax.fori_loop(count * i // of, count * (i + 1) // of, work, 0)

            return task

        def forward_piece(i):
            def task():
                of = heads // 4 // PIECES
                lax.fori_loop(i * of, (i + 1) * of, forward, 0)
                pass_piece(resid, i)()

            return task

        def keep_rows():
            keep(resid).start()
            loads[1].wait()

        drive(
            [gather(links, halves, gcap, cap_base)],
            [forward_piece(i) for i in range(PIECES)]
            + [keep_rows]
            + [part_of(backward, i, 4) for i in range(4)],
        )

        def sort_out(i, carry):
            lanes = pl.ds(pl.multiple_of(i * 256, 256), 256)
            high = pl.ds(pl.multiple_of(half_width + i * 256, 256), 256)
            taken = [dkeys[:, lanes], dvalues[:, lanes], dkeys[:, high], dvalues[:, high]]
            blocks = [
                jnp.concatenate([one[64 * c : 64 * c + 64] for one in taken], axis=0)
                for c in range(2)
            ]
            blocks = [dot(perm_t[...], block).astype(BF) for block in blocks]
            gparts[:, :, :, :, lanes] = jnp.concatenate(blocks, axis=0).reshape(
                RING, RING, 2, 2 * CAP, 256
            )
            return carry

        lax.fori_loop(0, half_width // 256, sort_out, 0)

        grad_stream = scatter(
            links, halves, gparts, grad_land, grad_base
        )
        next(grad_stream)
        expert()
        drive([scatter(links, halves, parts, ret_land, ret_base), grad_stream])
        grad_out[...] = scattered(gparts, (x, y, z), grad_land)
        finish(resid)
        keep(resid).wait()
        links.finish()


def place_rows(
    base, before, own_rows, their_rows, own_slot, their_slot, grad, layer_out, arriving, grad_out
):
    upper = pl.program_id(0) >= pl.num_programs(0) // 2
    tokens, lanes = base.shape
    row = lax.broadcasted_iota(jnp.int32, (2 * CAP, tokens), 0) - jnp.where(upper, CAP, 0)
    for slots, rows, kept, target in (
        (own_slot[:1, :], own_rows, base, layer_out),
        (their_slot[:1, :], their_rows, before, arriving),
    ):
        chosen = jnp.where(row < 0, 0.0, (slots == row).astype(F32)).astype(BF)
        turned = chosen.astype(F32).T.astype(BF)
        free = (1.0 - jnp.sum(turned.astype(F32), axis=-1, keepdims=True)).astype(BF)
        for start in range(0, lanes, 256):
            part = slice(start, start + 256)
            moved = dot(turned, rows[:, part]).astype(BF)
            target[:, part] = moved + kept[:, part] * free
    total = jnp.where(upper, grad[CAP:, :], grad[:CAP, :])
    for r in range(grad_out.shape[0]):
        grad_out[r] = total[2 * r : 2 * r + 2]


def local(
    layer_in, memory, cotangent, norm_gain, attn_gain, expert_in, expert_out, slot_index, gate_prob
):
    sections = lax.axis_size("section")
    tokens, width = layer_in.shape[1:]
    rows = memory.shape[1]
    stash = rows * 2 * RING * RING
    ffw = expert_in.shape[2]
    half = width // 2
    heads = width // HD
    vmem = pl.BlockSpec(memory_space=pltpu.VMEM)
    anywhere = pl.BlockSpec(memory_space=pl.ANY)
    full = (RING, RING, 2, 2 * CAP, half)
    quarter = half // 4
    landing = [
        pltpu.VMEM((2, RING, 2, 2, 2 * CAP, quarter), BF),
        pltpu.VMEM((2, RING, 2, 2, 2 * CAP, 2 * quarter), BF),
        pltpu.VMEM((2, len(GROUP), 2 * CAP, 2 * quarter), BF),
    ]
    count = 2 * GATHER_KEYS + 2 * SCATTER_KEYS + PIECES + 2
    base, before, own_rows, their_rows, their_slot, grad = pl.pallas_call(
        lambda *refs: kernel(sections, *refs),
        out_shape=(
            jax.ShapeDtypeStruct((tokens, width), BF),
            jax.ShapeDtypeStruct((tokens, width), BF),
            jax.ShapeDtypeStruct((2 * CAP, half), BF),
            jax.ShapeDtypeStruct((2 * CAP, half), BF),
            jax.ShapeDtypeStruct((8, tokens), jnp.int32),
            jax.ShapeDtypeStruct((2 * CAP, half), F32),
        ),
        in_specs=[vmem, anywhere, anywhere, vmem, vmem, anywhere, anywhere, vmem, vmem],
        out_specs=(anywhere, anywhere, vmem, vmem, vmem, vmem),
        scratch_shapes=[
            pltpu.VMEM((tokens, width), BF),
            pltpu.VMEM((tokens, width), BF),
            pltpu.VMEM((ffw, width), BF),
            pltpu.VMEM((ffw, width), BF),
            pltpu.VMEM((tokens, width), BF),
            pltpu.VMEM((tokens, width), BF),
            pltpu.VMEM(full, BF),
            pltpu.VMEM((stash, width), BF),
            pltpu.VMEM((stash, width), BF),
            pltpu.VMEM(full, BF),
            pltpu.VMEM((heads, stash, tokens), F32),
            pltpu.VMEM(full, BF),
            pltpu.VMEM(full, BF),
            pltpu.VMEM((stash, width), BF),
            pltpu.VMEM((stash, width), BF),
            pltpu.VMEM((2 * CAP, width), BF),
            pltpu.VMEM((2 * CAP, width), BF),
            pltpu.VMEM((2 * CAP, width), F32),
            pltpu.VMEM((256, 256), BF),
            pltpu.VMEM((256, 256), BF),
            pltpu.VMEM((ffw, 2 * RING * RING * CAP), F32),
            pltpu.VMEM((2 * RING * RING * CAP, ffw), BF),
            pltpu.VMEM((8, tokens), jnp.int32),
            *landing,
            *landing,
            pltpu.SemaphoreType.DMA((6,)),
            pltpu.SemaphoreType.DMA((count,)),
            pltpu.SemaphoreType.DMA((count,)),
        ],
        compiler_params=pltpu.CompilerParams(
            collective_id=0, has_side_effects=True, vmem_limit_bytes=60 * 1024 * 1024
        ),
    )(
        memory[0],
        layer_in[0],
        cotangent[0],
        norm_gain,
        attn_gain,
        expert_in[0].T,
        expert_out[0],
        slot_index,
        gate_prob,
    )
    steps = 2
    lanes = width // steps
    whole = pl.BlockSpec((tokens, lanes), lambda i: (0, i))
    folded = pl.BlockSpec((2 * CAP, lanes), lambda i: (0, i % (steps // 2)))
    layer_out, arriving, grad_memory = pl.pallas_call(
        place_rows,
        grid=(steps,),
        out_shape=(
            jax.ShapeDtypeStruct((tokens, width), BF),
            jax.ShapeDtypeStruct((tokens, width), BF),
            jax.ShapeDtypeStruct((rows, 2, width), F32),
        ),
        in_specs=[
            whole,
            whole,
            folded,
            folded,
            pl.BlockSpec((1, tokens), lambda i: (0, 0)),
            pl.BlockSpec((8, tokens), lambda i: (0, 0)),
            folded,
        ],
        out_specs=(whole, whole, pl.BlockSpec((rows, 2, lanes), lambda i: (0, 0, i))),
    )(base, before, own_rows, their_rows, slot_index, their_slot, grad)
    return (layer_out[None], arriving[None], grad_memory[None])


def solution(mesh):
    placed = (
        P("section", "expert", None),
        P("section", "expert", None, None),
        P("section", "expert", None),
        P("section", None),
        P("section", None),
        P("section", None, "expert"),
        P("section", "expert", None),
        P("section", "expert"),
        P("section", "expert"),
    )
    return jax.shard_map(
        local,
        mesh=mesh,
        in_specs=placed,
        out_specs=(
            P("section", "expert", None),
            P("section", "expert", None),
            P("section", "expert", None, None),
        ),
        check_vma=False,
    )
```

```python
import jax
import jax.numpy as jnp
from jax import lax
from jax.experimental import pallas as pl
from jax.experimental.pallas import tpu as pltpu
from jax.sharding import PartitionSpec as P

HD = 128
CAP = 8
RING = 4
MESH = pl.DeviceIdType.MESH
BF = jnp.bfloat16
F32 = jnp.float32
NT = (((1,), (1,)), ((), ()))
TN = (((0,), (0,)), ((), ()))


def dot(a, b, dims=(((1,), (0,)), ((), ()))):
    return lax.dot_general(a, b, dims, preferred_element_type=F32)


class Links:
    def __init__(self, send, recv, section, x, y, z):
        self.send, self.recv = send, recv
        self.section, self.x, self.y, self.z = section, x, y, z
        self.started = []

    def copy(self, key, src, dst, device):
        return pltpu.make_async_remote_copy(
            src_ref=src,
            dst_ref=dst,
            send_sem=self.send.at[key],
            recv_sem=self.recv.at[key],
            device_id=device,
            device_id_type=MESH,
        )

    def put(self, key, src, dst, device):
        copy = self.copy(key, src, dst, device)
        copy.start()
        self.started.append(copy)

    def got(self, key, dst, device):
        self.copy(key, dst, dst, device).wait_recv()

    def finish(self):
        for copy in self.started:
            copy.wait_send()
        self.started = []


GROUP = ((2, 0), (2, 1), (1, 0), (3, 0), (1, 1), (3, 1), (0, 1))


class Half:
    def __init__(self, links, first, lane, width):
        self.links, self.first, self.lane, self.width = links, first, lane, width
        self.u, self.v = (links.x, links.y) if first == "x" else (links.y, links.x)

    def at(self, buf, u, v, low=0, size=None):
        lanes = pl.ds(self.lane + low, self.width if size is None else size)
        if self.first == "x":
            return buf.at[u, v, :, :, lanes]
        return buf.at[v, u, :, :, lanes]

    def one(self, buf, u, v, z, low=0, size=None):
        lanes = pl.ds(self.lane + low, self.width if size is None else size)
        if self.first == "x":
            return buf.at[u, v, z, :, lanes]
        return buf.at[v, u, z, :, lanes]

    def device(self, u, v, z=None):
        x, y = (u, v) if self.first == "x" else (v, u)
        z = self.links.z if z is None else z
        return (self.links.section, x * (RING * 2) + y * 2 + z)


def step(i, by):
    return lax.rem(i + by + RING, RING)


GATHER_KEYS = 78
SCATTER_KEYS = 46
PIECES = 1
TURNS = ((0, 1), (1, -1))


def gather(links, halves, buf, base):
    z = links.z
    keyed = [(half, base + 39 * i) for i, half in enumerate(halves)]

    def source(half, slot):
        if slot == 7:
            return half.u, z
        du, dz = GROUP[slot]
        return step(half.u, -du), (z + dz) % 2

    def spread(half, key, slot):
        u, zz = source(half, slot)
        part = half.one(buf, u, half.v, zz)
        for d, turn in TURNS:
            links.put(key + 7 + slot * 4 + d, part, part, half.device(half.u, step(half.v, turn)))

    def relay(slot):
        for half, key in keyed:
            q = half.width // 2
            u, zz = source(half, slot)
            k = key + 7 + slot * 4
            for d, turn in TURNS:
                left = step(half.v, -turn)
                links.got(k + d, half.one(buf, u, left, zz), half.device(half.u, left))
                part = half.one(buf, u, left, zz, d * q, q)
                links.put(k + 2 + d, part, part, half.device(half.u, step(half.v, turn)))

    for i, (du, dz) in enumerate(GROUP):
        for half, key in keyed:
            part = half.one(buf, half.u, half.v, z)
            links.put(key + i, part, part, half.device(step(half.u, du), half.v, (z + dz) % 2))
    for half, key in keyed:
        spread(half, key, 7)
    yield
    order = (6, 2, 3, 4, 5, 0, 1)
    for n, slot in enumerate(order):
        for half, key in keyed:
            u, zz = source(half, slot)
            links.got(key + slot, half.one(buf, u, half.v, zz), half.device(u, half.v, zz))
            spread(half, key, slot)
        if n == 3:
            relay(7)
            yield
    yield
    for n, slot in enumerate(order):
        relay(slot)
        if n in (3, 6):
            yield
    for slot in (7,) + order:
        for half, key in keyed:
            q = half.width // 2
            u, zz = source(half, slot)
            for d, turn in TURNS:
                links.got(
                    key + 7 + slot * 4 + 2 + d,
                    half.one(buf, u, step(half.v, 2), zz, d * q, q),
                    half.device(half.u, step(half.v, -turn)),
                )


def add_into(target, *others):
    total = target[...].astype(F32)
    for other in others:
        total = total + other[...].astype(F32)
    target[...] = total.astype(target.dtype)


def scatter(links, halves, buf, land, base):
    passing, whole, last = land
    z = links.z
    order = ((0, 2), (1, -1), (2, 1), (3, 0))
    keyed = [(i, half, base + 23 * i) for i, half in enumerate(halves)]
    for slot, by in order:
        for i, half, key in keyed:
            q = half.width // 2
            for d, turn in TURNS:
                links.put(
                    key + slot * 4 + d,
                    half.at(buf, step(half.u, by), step(half.v, 2), d * q, q),
                    passing.at[i, slot, d],
                    half.device(half.u, step(half.v, turn)),
                )
    yield
    for slot, by in order:
        for i, half, key in keyed:
            q = half.width // 2
            for d, turn in TURNS:
                to = step(half.v, turn)
                links.got(
                    key + slot * 4 + d,
                    passing.at[i, slot, d],
                    half.device(half.u, step(half.v, -turn)),
                )
                add_into(half.at(buf, step(half.u, by), to, d * q, q), passing.at[i, slot, d])
                links.put(
                    key + slot * 4 + 2 + d,
                    half.at(buf, step(half.u, by), to),
                    whole.at[i, slot, d],
                    half.device(half.u, to),
                )
        yield
    for slot, by in order:
        for i, half, key in keyed:
            for d, turn in TURNS:
                links.got(
                    key + slot * 4 + 2 + d,
                    whole.at[i, slot, d],
                    half.device(half.u, step(half.v, -turn)),
                )
            add_into(
                half.at(buf, step(half.u, by), half.v),
                whole.at[i, slot, 0],
                whole.at[i, slot, 1],
            )
            for j, (du, dz) in enumerate(GROUP):
                if du == by % RING:
                    u, zz = step(half.u, du), (z + dz) % 2
                    links.put(
                        key + 16 + j,
                        half.one(buf, u, half.v, zz),
                        last.at[i, j],
                        half.device(u, half.v, zz),
                    )
        yield
    for i, half, key in keyed:
        for j, (du, dz) in enumerate(GROUP):
            u, zz = step(half.u, -du), (z + dz) % 2
            links.got(key + 16 + j, last.at[i, j], half.device(u, half.v, zz))


def scattered(buf, place, land):
    last = land[2]
    total = buf[place].astype(F32)
    others = [jnp.sum(last[i].astype(F32), axis=0) for i in range(2)]
    return total + jnp.concatenate(others, axis=1)


def drive(streams, tasks=()):
    streams, tasks = list(streams), list(tasks)
    while streams or tasks:
        for stream in list(streams):
            if next(stream, "end") == "end":
                streams.remove(stream)
        if tasks:
            tasks.pop(0)()


def scaled(rows, gain):
    return rows * lax.rsqrt(jnp.mean(rows * rows, axis=-1, keepdims=True) + 1e-06) * gain


def kernel(
    sections,
    mem_ref,
    layer_ref,
    cot_ref,
    norm_ref,
    attn_ref,
    in_ref,
    out_ref,
    slot_ref,
    gate_ref,
    base_out,
    before,
    own_rows,
    their_rows,
    their_slot,
    grad_out,
    cur,
    cot,
    win,
    wout,
    queries,
    resid,
    gkv,
    keys,
    values,
    gcap,
    probs,
    parts,
    gparts,
    dkeys,
    dvalues,
    picked,
    pickedq,
    attended,
    perm,
    perm_t,
    hacc,
    hidden,
    own_slot,
    land_a,
    land_b,
    land_c,
    gland_a,
    gland_b,
    gland_c,
    load_sem,
    send_sem,
    recv_sem,
):
    tokens, width = cur.shape
    half_width = width // 2
    heads = width // HD
    ffw = win.shape[0]
    scaling_factor = HD ** (-0.5)
    section = lax.axis_index("section")
    place = lax.axis_index("expert")
    x, y, z = place // (RING * 2), (place // 2) % RING, place % 2
    links = Links(send_sem, recv_sem, section, x, y, z)
    halves = (
        Half(links, "x", 0, half_width // 2),
        Half(links, "y", half_width // 2, half_width // 2),
    )
    cap_base, kv_base = 0, GATHER_KEYS
    ret_base = kv_base + GATHER_KEYS
    grad_base = ret_base + SCATTER_KEYS
    pass_base = grad_base + SCATTER_KEYS

    loads = [
        pltpu.make_async_copy(src, dst, load_sem.at[i])
        for i, (src, dst) in enumerate(
            ((layer_ref, cur), (cot_ref, cot), (in_ref, win), (out_ref, wout))
        )
    ]
    for load in loads:
        load.start()

    def device(xx, yy, zz):
        return (section, xx * (RING * 2) + yy * 2 + zz)

    barrier = pltpu.get_barrier_semaphore()
    peers = [device(step(x, dx), y, (z + dz) % 2) for dx in range(RING) for dz in range(2) if dx or dz]
    peers += [device(x, step(y, dy), (z + dz) % 2) for dy in range(1, RING) for dz in range(2)]
    for peer in peers:
        pl.semaphore_signal(barrier, inc=1, device_id=peer, device_id_type=MESH)

    @pl.when(section > 0)
    def _():
        pl.semaphore_signal(
            barrier, inc=1, device_id=(section - 1, place), device_id_type=MESH
        )

    @pl.when(section < sections - 1)
    def _():
        pl.semaphore_signal(
            barrier, inc=1, device_id=(section + 1, place), device_id_type=MESH
        )

    ends = jnp.where(section > 0, 1, 0) + jnp.where(section < sections - 1, 1, 0)
    pl.semaphore_wait(barrier, len(peers) + ends)

    def pass_copy(key, src, dst):
        return links.copy(pass_base + key, src, dst, (section + 1, place))

    def pass_on(key, src, dst):
        @pl.when(section < sections - 1)
        def _():
            pass_copy(key, src, dst).start()

    def pass_sent(key, src, dst):
        @pl.when(section < sections - 1)
        def _():
            pass_copy(key, src, dst).wait_send()

    def pass_got(key, dst):
        @pl.when(section > 0)
        def _():
            links.copy(pass_base + key, dst, dst, (section - 1, place)).wait_recv()

    def piece(ref, i):
        return ref.at[:, pl.ds(i * (width // PIECES), width // PIECES)]

    def pass_piece(base, i):
        return lambda: pass_on(2 + i, piece(base, i), piece(before, i))

    slots = slot_ref[...]
    rows16 = lax.broadcasted_iota(jnp.int32, (2 * CAP, tokens), 0)
    onehot = (slots == rows16).astype(F32).astype(BF)
    has_row = jnp.sum((slots == rows16).astype(F32), axis=-1, keepdims=True)

    def pick(source, target):
        def one(i, carry):
            lanes = pl.ds(pl.multiple_of(i * 512, 512), 512)
            target[:, lanes] = dot(onehot, source[:, lanes]).astype(target.dtype)
            return carry

        lax.fori_loop(0, width // 512, one, 0)

    def fold(rows):
        return jnp.concatenate([rows[:CAP, :half_width], rows[:CAP, half_width:]], axis=0)

    def put_capacity():
        rows = picked[...].astype(F32)
        gcap[x, y, z] = fold(scaled(rows, norm_ref[...])).astype(BF)

    def expert():
        loads[2].wait()
        loads[3].wait()
        hacc[...] = jnp.zeros_like(hacc)

        def into(k, carry):
            lanes = pl.ds(pl.multiple_of(k * 512, 512), 512)
            block = gcap[:, :, :, :, lanes].reshape(-1, 2 * CAP, 512).astype(F32)
            low = block[:, :CAP].reshape(-1, 512).astype(BF)
            high = block[:, CAP:].reshape(-1, 512).astype(BF)
            high_lanes = pl.ds(pl.multiple_of(half_width + k * 512, 512), 512)
            hacc[...] += dot(win[:, lanes], low, NT) + dot(win[:, high_lanes], high, NT)
            return carry

        lax.fori_loop(0, half_width // 512, into, 0)
        hidden[...] = jax.nn.gelu(hacc[...]).T.astype(BF)

        def out(k, carry):
            lanes = pl.ds(pl.multiple_of(k * 512, 512), 512)
            high_lanes = pl.ds(pl.multiple_of(half_width + k * 512, 512), 512)
            low = dot(hidden[...], wout[:, lanes]).reshape(-1, CAP, 512)
            high = dot(hidden[...], wout[:, high_lanes]).reshape(-1, CAP, 512)
            block = jnp.concatenate([low, high], axis=1).astype(BF)
            parts[:, :, :, :, lanes] = block.reshape(RING, RING, 2, 2 * CAP, 512)
            return carry

        lax.fori_loop(0, half_width // 512, out, 0)

    ret_land = (land_a, land_b, land_c)
    grad_land = (gland_a, gland_b, gland_c)

    def finish(base):
        returned = scattered(parts, (x, y, z), ret_land)
        gates = jnp.sum(
            jnp.where(slots == rows16[:CAP], gate_ref[...], 0.0), axis=-1, keepdims=True
        )
        gates = jnp.concatenate([gates, gates], axis=0)
        own_rows[...] = (fold(picked[...].astype(F32)) + gates * returned).astype(BF)
        pass_on(0, own_rows, their_rows)
        for i in range(PIECES):
            pass_got(2 + i, piece(before, i))
        pass_got(1, their_slot)
        pass_got(0, their_rows)

        for i in range(PIECES):
            pass_sent(2 + i, piece(base, i), piece(before, i))
        pass_sent(1, own_slot, their_slot)
        pass_sent(0, own_rows, their_rows)

    own_slot[...] = jnp.broadcast_to(slots, own_slot.shape)
    nothing = pltpu.make_async_copy(resid, before, load_sem.at[5])

    def keep(base):
        return pltpu.make_async_copy(base, base_out, load_sem.at[4])

    @pl.when(section < sections // 2)
    def _():
        loads[0].wait()
        pick(cur, picked)
        put_capacity()
        stream = gather(links, halves, gcap, cap_base)
        next(stream)
        pass_on(1, own_slot, their_slot)
        keep(cur).start()

        @pl.when(section == 0)
        def _():
            resid[...] = jnp.zeros_like(resid)
            nothing.start()
            their_slot[...] = jnp.full_like(their_slot, -1)
            their_rows[...] = jnp.zeros_like(their_rows)

        drive([stream])
        loads[1].wait()
        expert()
        pass_piece(cur, 0)()
        drive([scatter(links, halves, parts, ret_land, ret_base)])
        grad_out[...] = jnp.zeros_like(grad_out)
        finish(cur)
        keep(cur).wait()

        @pl.when(section == 0)
        def _():
            nothing.wait()

        links.finish()

    @pl.when(section >= sections // 2)
    def _():
        rows = [mem_ref[r].astype(F32) for r in range(mem_ref.shape[0])]
        gkv[x, y, z] = fold(jnp.concatenate(rows, axis=0)).astype(BF)

        def make_perm():
            for target, flip in ((perm, 0), (perm_t, 1)):
                k = lax.broadcasted_iota(jnp.int32, (256, 256), flip)
                i = lax.broadcasted_iota(jnp.int32, (256, 256), 1 - flip)
                m = k & 63
                source = ((m >> 2) << 4) + ((k >> 7) << 3) + ((m & 3) << 1) + ((k >> 6) & 1)
                target[...] = (source == i).astype(F32).astype(BF)

        def make_queries():
            loads[0].wait()

            def one(i, carry):
                rows = pl.ds(pl.multiple_of(i * 16, 16), 16)
                queries[rows, :] = scaled(cur[rows, :].astype(F32), attn_ref[...]).astype(BF)
                return carry

            lax.fori_loop(0, tokens // 16, one, 0)

        def pick_rows():
            pick(cur, picked)
            pick(queries, pickedq)

        drive(
            [gather(links, halves, gkv, kv_base)],
            [lambda: pass_on(1, own_slot, their_slot), make_perm, make_queries, pick_rows],
        )

        def sort_in(i, carry):
            lanes = pl.ds(pl.multiple_of(i * 512, 512), 512)
            high = pl.ds(pl.multiple_of(half_width + i * 512, 512), 512)
            blocks = [gkv[2 * c : 2 * c + 2, :, :, :, lanes].reshape(256, 512) for c in range(2)]
            blocks = [dot(perm[...], block).astype(BF) for block in blocks]
            for start, target, place in (
                (0, keys, lanes),
                (64, values, lanes),
                (128, keys, high),
                (192, values, high),
            ):
                target[:, place] = jnp.concatenate(
                    [block[start : start + 64] for block in blocks], axis=0
                )
            return carry

        lax.fori_loop(0, half_width // 512, sort_in, 0)

        def heads_of(block, count):
            return [block[:, j * HD : (j + 1) * HD] for j in range(count)]

        def chosen_heads(group, carry):
            lanes = pl.ds(pl.multiple_of(group * (20 * HD), 20 * HD), 20 * HD)
            asked, kept = heads_of(pickedq[:, lanes], 20), heads_of(keys[:, lanes], 20)
            scores = [dot(q, k, NT) for q, k in zip(asked, kept)]
            scores = jnp.concatenate(scores, axis=0) * scaling_factor
            weights = jnp.exp(scores - jnp.max(scores, axis=-1, keepdims=True))
            weights = (weights / jnp.sum(weights, axis=-1, keepdims=True)).astype(BF)
            mixed = [
                dot(weights[2 * CAP * j : 2 * CAP * (j + 1)], v)
                for j, v in enumerate(heads_of(values[:, lanes], 20))
            ]
            mixed = jnp.concatenate(mixed, axis=1)
            attended[:, lanes] = picked[:, lanes].astype(F32) + mixed * has_row
            return carry

        lax.fori_loop(0, heads // 20, chosen_heads, 0)
        picked[...] = attended[...].astype(BF)
        put_capacity()

        def forward(group, carry):
            lanes = pl.ds(pl.multiple_of(group * (8 * HD), 8 * HD), 8 * HD)
            asked, kept = heads_of(queries[:, lanes], 8), heads_of(keys[:, lanes], 8)
            scores = [dot(k, q, NT) * scaling_factor for q, k in zip(asked, kept)]
            weights = [jnp.exp(one - jnp.max(one, axis=0, keepdims=True)) for one in scores]
            weights = [one / jnp.sum(one, axis=0, keepdims=True) for one in weights]
            mixed = [
                dot(one.astype(BF), v, TN)
                for one, v in zip(weights, heads_of(values[:, lanes], 8))
            ]
            mixed = jnp.concatenate(mixed, axis=1)
            resid[:, lanes] = (cur[:, lanes].astype(F32) + mixed).astype(BF)
            for j, one in enumerate(weights):
                probs[group * 8 + j] = one
            return carry

        def backward(group, carry):
            lanes = pl.ds(pl.multiple_of(group * (8 * HD), 8 * HD), 8 * HD)
            weights = [probs[group * 8 + j] for j in range(8)]
            upstream, asked = heads_of(cot[:, lanes], 8), heads_of(queries[:, lanes], 8)
            dweights = [dot(v, g, NT) for v, g in zip(heads_of(values[:, lanes], 8), upstream)]
            inner = [
                jnp.sum(d * one, axis=0, keepdims=True) for d, one in zip(dweights, weights)
            ]
            dscores = [
                one * (d - i) * scaling_factor for one, d, i in zip(weights, dweights, inner)
            ]
            high = [one.astype(BF) for one in dscores]
            low = [(one - h.astype(F32)).astype(BF) for one, h in zip(dscores, high)]
            dk = [
                dot(jnp.concatenate([h, l], axis=1), jnp.concatenate([q, q], axis=0))
                for h, l, q in zip(high, low, asked)
            ]
            dv = [dot(one.astype(BF), g) for one, g in zip(weights, upstream)]
            dkeys[:, lanes] = jnp.concatenate(dk, axis=1).astype(BF)
            dvalues[:, lanes] = jnp.concatenate(dv, axis=1).astype(BF)
            return carry

        def part_of(work, i, of):
            count = heads // 8

            def task():
                lax.fori_loop(count * i // of, count * (i + 1) // of, work, 0)

            return task

        def forward_piece(i):
            def task():
                of = heads // 8 // PIECES
                lax.fori_loop(i * of, (i + 1) * of, forward, 0)
                pass_piece(resid, i)()

            return task

        def keep_rows():
            keep(resid).start()
            loads[1].wait()

        drive(
            [gather(links, halves, gcap, cap_base)],
            [forward_piece(i) for i in range(PIECES)]
            + [keep_rows]
            + [part_of(backward, i, 4) for i in range(4)],
        )

        def sort_out(i, carry):
            lanes = pl.ds(pl.multiple_of(i * 512, 512), 512)
            high = pl.ds(pl.multiple_of(half_width + i * 512, 512), 512)
            taken = [dkeys[:, lanes], dvalues[:, lanes], dkeys[:, high], dvalues[:, high]]
            blocks = [
                jnp.concatenate([one[64 * c : 64 * c + 64] for one in taken], axis=0)
                for c in range(2)
            ]
            blocks = [dot(perm_t[...], block).astype(BF) for block in blocks]
            gparts[:, :, :, :, lanes] = jnp.concatenate(blocks, axis=0).reshape(
                RING, RING, 2, 2 * CAP, 512
            )
            return carry

        lax.fori_loop(0, half_width // 512, sort_out, 0)

        grad_stream = scatter(
            links, halves, gparts, grad_land, grad_base
        )
        next(grad_stream)
        expert()
        drive([scatter(links, halves, parts, ret_land, ret_base), grad_stream])
        grad_out[...] = scattered(gparts, (x, y, z), grad_land)
        finish(resid)
        keep(resid).wait()
        links.finish()


def place_rows(
    base, before, own_rows, their_rows, own_slot, their_slot, grad, layer_out, arriving, grad_out
):
    upper = pl.program_id(0) >= pl.num_programs(0) // 2
    tokens, lanes = base.shape
    row = lax.broadcasted_iota(jnp.int32, (2 * CAP, tokens), 0) - jnp.where(upper, CAP, 0)
    for slots, rows, kept, target in (
        (own_slot[:1, :], own_rows, base, layer_out),
        (their_slot[:1, :], their_rows, before, arriving),
    ):
        chosen = jnp.where(row < 0, 0.0, (slots == row).astype(F32)).astype(BF)
        turned = chosen.astype(F32).T.astype(BF)
        free = (1.0 - jnp.sum(turned.astype(F32), axis=-1, keepdims=True)).astype(BF)
        for start in range(0, lanes, 256):
            part = slice(start, start + 256)
            moved = dot(turned, rows[:, part]).astype(BF)
            target[:, part] = moved + kept[:, part] * free
    total = jnp.where(upper, grad[CAP:, :], grad[:CAP, :])
    for r in range(grad_out.shape[0]):
        grad_out[r] = total[2 * r : 2 * r + 2]


def local(
    layer_in, memory, cotangent, norm_gain, attn_gain, expert_in, expert_out, slot_index, gate_prob
):
    sections = lax.axis_size("section")
    tokens, width = layer_in.shape[1:]
    rows = memory.shape[1]
    stash = rows * 2 * RING * RING
    ffw = expert_in.shape[2]
    half = width // 2
    heads = width // HD
    vmem = pl.BlockSpec(memory_space=pltpu.VMEM)
    anywhere = pl.BlockSpec(memory_space=pl.ANY)
    full = (RING, RING, 2, 2 * CAP, half)
    quarter = half // 4
    landing = [
        pltpu.VMEM((2, RING, 2, 2, 2 * CAP, quarter), BF),
        pltpu.VMEM((2, RING, 2, 2, 2 * CAP, 2 * quarter), BF),
        pltpu.VMEM((2, len(GROUP), 2 * CAP, 2 * quarter), BF),
    ]
    count = 2 * GATHER_KEYS + 2 * SCATTER_KEYS + PIECES + 2
    base, before, own_rows, their_rows, their_slot, grad = pl.pallas_call(
        lambda *refs: kernel(sections, *refs),
        out_shape=(
            jax.ShapeDtypeStruct((tokens, width), BF),
            jax.ShapeDtypeStruct((tokens, width), BF),
            jax.ShapeDtypeStruct((2 * CAP, half), BF),
            jax.ShapeDtypeStruct((2 * CAP, half), BF),
            jax.ShapeDtypeStruct((8, tokens), jnp.int32),
            jax.ShapeDtypeStruct((2 * CAP, half), F32),
        ),
        in_specs=[vmem, anywhere, anywhere, vmem, vmem, anywhere, anywhere, vmem, vmem],
        out_specs=(anywhere, anywhere, vmem, vmem, vmem, vmem),
        scratch_shapes=[
            pltpu.VMEM((tokens, width), BF),
            pltpu.VMEM((tokens, width), BF),
            pltpu.VMEM((ffw, width), BF),
            pltpu.VMEM((ffw, width), BF),
            pltpu.VMEM((tokens, width), BF),
            pltpu.VMEM((tokens, width), BF),
            pltpu.VMEM(full, BF),
            pltpu.VMEM((stash, width), BF),
            pltpu.VMEM((stash, width), BF),
            pltpu.VMEM(full, BF),
            pltpu.VMEM((heads, stash, tokens), F32),
            pltpu.VMEM(full, BF),
            pltpu.VMEM(full, BF),
            pltpu.VMEM((stash, width), BF),
            pltpu.VMEM((stash, width), BF),
            pltpu.VMEM((2 * CAP, width), BF),
            pltpu.VMEM((2 * CAP, width), BF),
            pltpu.VMEM((2 * CAP, width), F32),
            pltpu.VMEM((256, 256), BF),
            pltpu.VMEM((256, 256), BF),
            pltpu.VMEM((ffw, 2 * RING * RING * CAP), F32),
            pltpu.VMEM((2 * RING * RING * CAP, ffw), BF),
            pltpu.VMEM((8, tokens), jnp.int32),
            *landing,
            *landing,
            pltpu.SemaphoreType.DMA((6,)),
            pltpu.SemaphoreType.DMA((count,)),
            pltpu.SemaphoreType.DMA((count,)),
        ],
        compiler_params=pltpu.CompilerParams(
            collective_id=0, has_side_effects=True, vmem_limit_bytes=60 * 1024 * 1024
        ),
    )(
        memory[0],
        layer_in[0],
        cotangent[0],
        norm_gain,
        attn_gain,
        expert_in[0].T,
        expert_out[0],
        slot_index,
        gate_prob,
    )
    steps = 2
    lanes = width // steps
    whole = pl.BlockSpec((tokens, lanes), lambda i: (0, i))
    folded = pl.BlockSpec((2 * CAP, lanes), lambda i: (0, i % (steps // 2)))
    layer_out, arriving, grad_memory = pl.pallas_call(
        place_rows,
        grid=(steps,),
        out_shape=(
            jax.ShapeDtypeStruct((tokens, width), BF),
            jax.ShapeDtypeStruct((tokens, width), BF),
            jax.ShapeDtypeStruct((rows, 2, width), F32),
        ),
        in_specs=[
            whole,
            whole,
            folded,
            folded,
            pl.BlockSpec((1, tokens), lambda i: (0, 0)),
            pl.BlockSpec((8, tokens), lambda i: (0, 0)),
            folded,
        ],
        out_specs=(whole, whole, pl.BlockSpec((rows, 2, lanes), lambda i: (0, 0, i))),
    )(base, before, own_rows, their_rows, slot_index, their_slot, grad)
    return (layer_out[None], arriving[None], grad_memory[None])


def solution(mesh):
    placed = (
        P("section", "expert", None),
        P("section", "expert", None, None),
        P("section", "expert", None),
        P("section", None),
        P("section", None),
        P("section", None, "expert"),
        P("section", "expert", None),
        P("section", "expert"),
        P("section", "expert"),
    )
    return jax.shard_map(
        local,
        mesh=mesh,
        in_specs=placed,
        out_specs=(
            P("section", "expert", None),
            P("section", "expert", None),
            P("section", "expert", None, None),
        ),
        check_vma=False,
    )
```

```python
import jax
import jax.numpy as jnp
from jax import lax
from jax.experimental import pallas as pl
from jax.experimental.pallas import tpu as pltpu
from jax.sharding import PartitionSpec as P

HD = 128
CAP = 8
RING = 4
MESH = pl.DeviceIdType.MESH
BF = jnp.bfloat16
F32 = jnp.float32
NT = (((1,), (1,)), ((), ()))
TN = (((0,), (0,)), ((), ()))


def dot(a, b, dims=(((1,), (0,)), ((), ()))):
    return lax.dot_general(a, b, dims, preferred_element_type=F32)


class Links:
    def __init__(self, send, recv, section, x, y, z):
        self.send, self.recv = send, recv
        self.section, self.x, self.y, self.z = section, x, y, z
        self.started = []

    def copy(self, key, src, dst, device):
        return pltpu.make_async_remote_copy(
            src_ref=src,
            dst_ref=dst,
            send_sem=self.send.at[key],
            recv_sem=self.recv.at[key],
            device_id=device,
            device_id_type=MESH,
        )

    def put(self, key, src, dst, device):
        copy = self.copy(key, src, dst, device)
        copy.start()
        self.started.append(copy)

    def got(self, key, dst, device):
        self.copy(key, dst, dst, device).wait_recv()

    def finish(self):
        for copy in self.started:
            copy.wait_send()
        self.started = []


GROUP = ((2, 0), (2, 1), (1, 0), (3, 0), (1, 1), (3, 1), (0, 1))


class Half:
    def __init__(self, links, first, lane, width):
        self.links, self.first, self.lane, self.width = links, first, lane, width
        self.u, self.v = (links.x, links.y) if first == "x" else (links.y, links.x)

    def at(self, buf, u, v, low=0, size=None):
        lanes = pl.ds(self.lane + low, self.width if size is None else size)
        if self.first == "x":
            return buf.at[u, v, :, :, lanes]
        return buf.at[v, u, :, :, lanes]

    def one(self, buf, u, v, z, low=0, size=None):
        lanes = pl.ds(self.lane + low, self.width if size is None else size)
        if self.first == "x":
            return buf.at[u, v, z, :, lanes]
        return buf.at[v, u, z, :, lanes]

    def device(self, u, v, z=None):
        x, y = (u, v) if self.first == "x" else (v, u)
        z = self.links.z if z is None else z
        return (self.links.section, x * (RING * 2) + y * 2 + z)


def step(i, by):
    return lax.rem(i + by + RING, RING)


GATHER_KEYS = 78
SCATTER_KEYS = 46
PIECES = 1
TURNS = ((0, 1), (1, -1))


def gather(links, halves, buf, base):
    z = links.z
    keyed = [(half, base + 39 * i) for i, half in enumerate(halves)]

    def source(half, slot):
        if slot == 7:
            return half.u, z
        du, dz = GROUP[slot]
        return step(half.u, -du), (z + dz) % 2

    def spread(half, key, slot):
        u, zz = source(half, slot)
        part = half.one(buf, u, half.v, zz)
        for d, turn in TURNS:
            links.put(key + 7 + slot * 4 + d, part, part, half.device(half.u, step(half.v, turn)))

    def relay(slot):
        for half, key in keyed:
            q = half.width // 2
            u, zz = source(half, slot)
            k = key + 7 + slot * 4
            for d, turn in TURNS:
                left = step(half.v, -turn)
                links.got(k + d, half.one(buf, u, left, zz), half.device(half.u, left))
                part = half.one(buf, u, left, zz, d * q, q)
                links.put(k + 2 + d, part, part, half.device(half.u, step(half.v, turn)))

    for i, (du, dz) in enumerate(GROUP):
        for half, key in keyed:
            part = half.one(buf, half.u, half.v, z)
            links.put(key + i, part, part, half.device(step(half.u, du), half.v, (z + dz) % 2))
    for half, key in keyed:
        spread(half, key, 7)
    yield
    order = (6, 2, 3, 4, 5, 0, 1)
    for n, slot in enumerate(order):
        for half, key in keyed:
            u, zz = source(half, slot)
            links.got(key + slot, half.one(buf, u, half.v, zz), half.device(u, half.v, zz))
            spread(half, key, slot)
        if n == 3:
            relay(7)
            yield
    yield
    for n, slot in enumerate(order):
        relay(slot)
        if n in (3, 6):
            yield
    for slot in (7,) + order:
        for half, key in keyed:
            q = half.width // 2
            u, zz = source(half, slot)
            for d, turn in TURNS:
                links.got(
                    key + 7 + slot * 4 + 2 + d,
                    half.one(buf, u, step(half.v, 2), zz, d * q, q),
                    half.device(half.u, step(half.v, -turn)),
                )


def add_into(target, *others):
    total = target[...].astype(F32)
    for other in others:
        total = total + other[...].astype(F32)
    target[...] = total.astype(target.dtype)


def scatter(links, halves, buf, land, base):
    passing, whole, last = land
    z = links.z
    order = ((0, 2), (1, -1), (2, 1), (3, 0))
    keyed = [(i, half, base + 23 * i) for i, half in enumerate(halves)]
    for slot, by in order:
        for i, half, key in keyed:
            q = half.width // 2
            for d, turn in TURNS:
                links.put(
                    key + slot * 4 + d,
                    half.at(buf, step(half.u, by), step(half.v, 2), d * q, q),
                    passing.at[i, slot, d],
                    half.device(half.u, step(half.v, turn)),
                )
    yield
    for slot, by in order:
        for i, half, key in keyed:
            q = half.width // 2
            for d, turn in TURNS:
                to = step(half.v, turn)
                links.got(
                    key + slot * 4 + d,
                    passing.at[i, slot, d],
                    half.device(half.u, step(half.v, -turn)),
                )
                add_into(half.at(buf, step(half.u, by), to, d * q, q), passing.at[i, slot, d])
                links.put(
                    key + slot * 4 + 2 + d,
                    half.at(buf, step(half.u, by), to),
                    whole.at[i, slot, d],
                    half.device(half.u, to),
                )
        yield
    for slot, by in order:
        for i, half, key in keyed:
            for d, turn in TURNS:
                links.got(
                    key + slot * 4 + 2 + d,
                    whole.at[i, slot, d],
                    half.device(half.u, step(half.v, -turn)),
                )
            add_into(
                half.at(buf, step(half.u, by), half.v),
                whole.at[i, slot, 0],
                whole.at[i, slot, 1],
            )
            for j, (du, dz) in enumerate(GROUP):
                if du == by % RING:
                    u, zz = step(half.u, du), (z + dz) % 2
                    links.put(
                        key + 16 + j,
                        half.one(buf, u, half.v, zz),
                        last.at[i, j],
                        half.device(u, half.v, zz),
                    )
        yield
    for i, half, key in keyed:
        for j, (du, dz) in enumerate(GROUP):
            u, zz = step(half.u, -du), (z + dz) % 2
            links.got(key + 16 + j, last.at[i, j], half.device(u, half.v, zz))


def scattered(buf, place, land):
    last = land[2]
    total = buf[place].astype(F32)
    others = [jnp.sum(last[i].astype(F32), axis=0) for i in range(2)]
    return total + jnp.concatenate(others, axis=1)


def drive(streams, tasks=()):
    streams, tasks = list(streams), list(tasks)
    while streams or tasks:
        for stream in list(streams):
            if next(stream, "end") == "end":
                streams.remove(stream)
        if tasks:
            tasks.pop(0)()


def scaled(rows, gain):
    return rows * lax.rsqrt(jnp.mean(rows * rows, axis=-1, keepdims=True) + 1e-06) * gain


def kernel(
    sections,
    mem_ref,
    layer_ref,
    cot_ref,
    norm_ref,
    attn_ref,
    in_ref,
    out_ref,
    slot_ref,
    gate_ref,
    base_out,
    before,
    own_rows,
    their_rows,
    their_slot,
    grad_out,
    cur,
    cot,
    win,
    wout,
    queries,
    resid,
    gkv,
    keys,
    values,
    gcap,
    probs,
    parts,
    gparts,
    dkeys,
    dvalues,
    picked,
    pickedq,
    attended,
    perm,
    perm_t,
    hacc,
    hidden,
    own_slot,
    land_a,
    land_b,
    land_c,
    gland_a,
    gland_b,
    gland_c,
    load_sem,
    send_sem,
    recv_sem,
):
    tokens, width = cur.shape
    half_width = width // 2
    heads = width // HD
    ffw = win.shape[0]
    scaling_factor = HD ** (-0.5)
    section = lax.axis_index("section")
    place = lax.axis_index("expert")
    x, y, z = place // (RING * 2), (place // 2) % RING, place % 2
    links = Links(send_sem, recv_sem, section, x, y, z)
    halves = (
        Half(links, "x", 0, half_width // 2),
        Half(links, "y", half_width // 2, half_width // 2),
    )
    cap_base, kv_base = 0, GATHER_KEYS
    ret_base = kv_base + GATHER_KEYS
    grad_base = ret_base + SCATTER_KEYS
    pass_base = grad_base + SCATTER_KEYS

    loads = [
        pltpu.make_async_copy(src, dst, load_sem.at[i])
        for i, (src, dst) in enumerate(
            ((layer_ref, cur), (cot_ref, cot), (in_ref, win), (out_ref, wout))
        )
    ]
    for load in loads:
        load.start()

    def device(xx, yy, zz):
        return (section, xx * (RING * 2) + yy * 2 + zz)

    barrier = pltpu.get_barrier_semaphore()
    peers = [device(step(x, dx), y, (z + dz) % 2) for dx in range(RING) for dz in range(2) if dx or dz]
    peers += [device(x, step(y, dy), (z + dz) % 2) for dy in range(1, RING) for dz in range(2)]
    for peer in peers:
        pl.semaphore_signal(barrier, inc=1, device_id=peer, device_id_type=MESH)

    @pl.when(section > 0)
    def _():
        pl.semaphore_signal(
            barrier, inc=1, device_id=(section - 1, place), device_id_type=MESH
        )

    @pl.when(section < sections - 1)
    def _():
        pl.semaphore_signal(
            barrier, inc=1, device_id=(section + 1, place), device_id_type=MESH
        )

    ends = jnp.where(section > 0, 1, 0) + jnp.where(section < sections - 1, 1, 0)
    pl.semaphore_wait(barrier, len(peers) + ends)

    def pass_copy(key, src, dst):
        return links.copy(pass_base + key, src, dst, (section + 1, place))

    def pass_on(key, src, dst):
        @pl.when(section < sections - 1)
        def _():
            pass_copy(key, src, dst).start()

    def pass_sent(key, src, dst):
        @pl.when(section < sections - 1)
        def _():
            pass_copy(key, src, dst).wait_send()

    def pass_got(key, dst):
        @pl.when(section > 0)
        def _():
            links.copy(pass_base + key, dst, dst, (section - 1, place)).wait_recv()

    def piece(ref, i):
        return ref.at[:, pl.ds(i * (width // PIECES), width // PIECES)]

    def pass_piece(base, i):
        return lambda: pass_on(2 + i, piece(base, i), piece(before, i))

    slots = slot_ref[...]
    rows16 = lax.broadcasted_iota(jnp.int32, (2 * CAP, tokens), 0)
    onehot = (slots == rows16).astype(F32).astype(BF)
    has_row = jnp.sum((slots == rows16).astype(F32), axis=-1, keepdims=True)

    def pick(source, target):
        def one(i, carry):
            lanes = pl.ds(pl.multiple_of(i * 1280, 1280), 1280)
            target[:, lanes] = dot(onehot, source[:, lanes]).astype(target.dtype)
            return carry

        lax.fori_loop(0, width // 1280, one, 0)

    def fold(rows):
        return jnp.concatenate([rows[:CAP, :half_width], rows[:CAP, half_width:]], axis=0)

    def put_capacity():
        rows = picked[...].astype(F32)
        gcap[x, y, z] = fold(scaled(rows, norm_ref[...])).astype(BF)

    def expert():
        loads[2].wait()
        loads[3].wait()
        hacc[...] = jnp.zeros_like(hacc)

        def into(k, carry):
            lanes = pl.ds(pl.multiple_of(k * 1280, 1280), 1280)
            block = gcap[:, :, :, :, lanes].reshape(-1, 2 * CAP, 1280).astype(F32)
            low = block[:, :CAP].reshape(-1, 1280).astype(BF)
            high = block[:, CAP:].reshape(-1, 1280).astype(BF)
            high_lanes = pl.ds(pl.multiple_of(half_width + k * 1280, 1280), 1280)
            hacc[...] += dot(win[:, lanes], low, NT) + dot(win[:, high_lanes], high, NT)
            return carry

        lax.fori_loop(0, half_width // 1280, into, 0)
        hidden[...] = jax.nn.gelu(hacc[...]).T.astype(BF)

        def out(k, carry):
            lanes = pl.ds(pl.multiple_of(k * 1280, 1280), 1280)
            high_lanes = pl.ds(pl.multiple_of(half_width + k * 1280, 1280), 1280)
            low = dot(hidden[...], wout[:, lanes]).reshape(-1, CAP, 1280)
            high = dot(hidden[...], wout[:, high_lanes]).reshape(-1, CAP, 1280)
            block = jnp.concatenate([low, high], axis=1).astype(BF)
            parts[:, :, :, :, lanes] = block.reshape(RING, RING, 2, 2 * CAP, 1280)
            return carry

        lax.fori_loop(0, half_width // 1280, out, 0)

    ret_land = (land_a, land_b, land_c)
    grad_land = (gland_a, gland_b, gland_c)

    def finish(base):
        returned = scattered(parts, (x, y, z), ret_land)
        gates = jnp.sum(
            jnp.where(slots == rows16[:CAP], gate_ref[...], 0.0), axis=-1, keepdims=True
        )
        gates = jnp.concatenate([gates, gates], axis=0)
        own_rows[...] = (fold(picked[...].astype(F32)) + gates * returned).astype(BF)
        pass_on(0, own_rows, their_rows)
        for i in range(PIECES):
            pass_got(2 + i, piece(before, i))
        pass_got(1, their_slot)
        pass_got(0, their_rows)

        for i in range(PIECES):
            pass_sent(2 + i, piece(base, i), piece(before, i))
        pass_sent(1, own_slot, their_slot)
        pass_sent(0, own_rows, their_rows)

    own_slot[...] = jnp.broadcast_to(slots, own_slot.shape)
    nothing = pltpu.make_async_copy(resid, before, load_sem.at[5])

    def keep(base):
        return pltpu.make_async_copy(base, base_out, load_sem.at[4])

    @pl.when(section < sections // 2)
    def _():
        loads[0].wait()
        pick(cur, picked)
        put_capacity()
        stream = gather(links, halves, gcap, cap_base)
        next(stream)
        pass_on(1, own_slot, their_slot)
        keep(cur).start()

        @pl.when(section == 0)
        def _():
            resid[...] = jnp.zeros_like(resid)
            nothing.start()
            their_slot[...] = jnp.full_like(their_slot, -1)
            their_rows[...] = jnp.zeros_like(their_rows)

        drive([stream])
        loads[1].wait()
        expert()
        pass_piece(cur, 0)()
        drive([scatter(links, halves, parts, ret_land, ret_base)])
        grad_out[...] = jnp.zeros_like(grad_out)
        finish(cur)
        keep(cur).wait()

        @pl.when(section == 0)
        def _():
            nothing.wait()

        links.finish()

    @pl.when(section >= sections // 2)
    def _():
        rows = [mem_ref[r].astype(F32) for r in range(mem_ref.shape[0])]
        gkv[x, y, z] = fold(jnp.concatenate(rows, axis=0)).astype(BF)

        def make_perm():
            for target, flip in ((perm, 0), (perm_t, 1)):
                k = lax.broadcasted_iota(jnp.int32, (256, 256), flip)
                i = lax.broadcasted_iota(jnp.int32, (256, 256), 1 - flip)
                m = k & 63
                source = ((m >> 2) << 4) + ((k >> 7) << 3) + ((m & 3) << 1) + ((k >> 6) & 1)
                target[...] = (source == i).astype(F32).astype(BF)

        def make_queries():
            loads[0].wait()

            def one(i, carry):
                rows = pl.ds(pl.multiple_of(i * 32, 32), 32)
                queries[rows, :] = scaled(cur[rows, :].astype(F32), attn_ref[...]).astype(BF)
                return carry

            lax.fori_loop(0, tokens // 32, one, 0)

        def pick_rows():
            pick(cur, picked)
            pick(queries, pickedq)

        drive(
            [gather(links, halves, gkv, kv_base)],
            [lambda: pass_on(1, own_slot, their_slot), make_perm, make_queries, pick_rows],
        )

        def sort_in(i, carry):
            lanes = pl.ds(pl.multiple_of(i * 512, 512), 512)
            high = pl.ds(pl.multiple_of(half_width + i * 512, 512), 512)
            blocks = [gkv[2 * c : 2 * c + 2, :, :, :, lanes].reshape(256, 512) for c in range(2)]
            blocks = [dot(perm[...], block).astype(BF) for block in blocks]
            for start, target, place in (
                (0, keys, lanes),
                (64, values, lanes),
                (128, keys, high),
                (192, values, high),
            ):
                target[:, place] = jnp.concatenate(
                    [block[start : start + 64] for block in blocks], axis=0
                )
            return carry

        lax.fori_loop(0, half_width // 512, sort_in, 0)

        def heads_of(block, count):
            return [block[:, j * HD : (j + 1) * HD] for j in range(count)]

        def chosen_heads(group, carry):
            lanes = pl.ds(pl.multiple_of(group * (20 * HD), 20 * HD), 20 * HD)
            asked, kept = heads_of(pickedq[:, lanes], 20), heads_of(keys[:, lanes], 20)
            scores = [dot(q, k, NT) for q, k in zip(asked, kept)]
            scores = jnp.concatenate(scores, axis=0) * scaling_factor
            weights = jnp.exp(scores - jnp.max(scores, axis=-1, keepdims=True))
            weights = (weights / jnp.sum(weights, axis=-1, keepdims=True)).astype(BF)
            mixed = [
                dot(weights[2 * CAP * j : 2 * CAP * (j + 1)], v)
                for j, v in enumerate(heads_of(values[:, lanes], 20))
            ]
            mixed = jnp.concatenate(mixed, axis=1)
            attended[:, lanes] = picked[:, lanes].astype(F32) + mixed * has_row
            return carry

        lax.fori_loop(0, heads // 20, chosen_heads, 0)
        picked[...] = attended[...].astype(BF)
        put_capacity()

        def forward(group, carry):
            lanes = pl.ds(pl.multiple_of(group * (8 * HD), 8 * HD), 8 * HD)
            asked, kept = heads_of(queries[:, lanes], 8), heads_of(keys[:, lanes], 8)
            scores = [dot(k, q, NT) * scaling_factor for q, k in zip(asked, kept)]
            weights = [jnp.exp(one - jnp.max(one, axis=0, keepdims=True)) for one in scores]
            weights = [one / jnp.sum(one, axis=0, keepdims=True) for one in weights]
            mixed = [
                dot(one.astype(BF), v, TN)
                for one, v in zip(weights, heads_of(values[:, lanes], 8))
            ]
            mixed = jnp.concatenate(mixed, axis=1)
            resid[:, lanes] = (cur[:, lanes].astype(F32) + mixed).astype(BF)
            for j, one in enumerate(weights):
                probs[group * 8 + j] = one
            return carry

        def backward(group, carry):
            lanes = pl.ds(pl.multiple_of(group * (8 * HD), 8 * HD), 8 * HD)
            weights = [probs[group * 8 + j] for j in range(8)]
            upstream, asked = heads_of(cot[:, lanes], 8), heads_of(queries[:, lanes], 8)
            dweights = [dot(v, g, NT) for v, g in zip(heads_of(values[:, lanes], 8), upstream)]
            inner = [
                jnp.sum(d * one, axis=0, keepdims=True) for d, one in zip(dweights, weights)
            ]
            dscores = [
                one * (d - i) * scaling_factor for one, d, i in zip(weights, dweights, inner)
            ]
            high = [one.astype(BF) for one in dscores]
            low = [(one - h.astype(F32)).astype(BF) for one, h in zip(dscores, high)]
            dk = [
                dot(jnp.concatenate([h, l], axis=1), jnp.concatenate([q, q], axis=0))
                for h, l, q in zip(high, low, asked)
            ]
            dv = [dot(one.astype(BF), g) for one, g in zip(weights, upstream)]
            dkeys[:, lanes] = jnp.concatenate(dk, axis=1).astype(BF)
            dvalues[:, lanes] = jnp.concatenate(dv, axis=1).astype(BF)
            return carry

        def part_of(work, i, of):
            count = heads // 8

            def task():
                lax.fori_loop(count * i // of, count * (i + 1) // of, work, 0)

            return task

        def forward_piece(i):
            def task():
                of = heads // 8 // PIECES
                lax.fori_loop(i * of, (i + 1) * of, forward, 0)
                pass_piece(resid, i)()

            return task

        def keep_rows():
            keep(resid).start()
            loads[1].wait()

        drive(
            [gather(links, halves, gcap, cap_base)],
            [forward_piece(i) for i in range(PIECES)]
            + [keep_rows]
            + [part_of(backward, i, 4) for i in range(4)],
        )

        def sort_out(i, carry):
            lanes = pl.ds(pl.multiple_of(i * 512, 512), 512)
            high = pl.ds(pl.multiple_of(half_width + i * 512, 512), 512)
            taken = [dkeys[:, lanes], dvalues[:, lanes], dkeys[:, high], dvalues[:, high]]
            blocks = [
                jnp.concatenate([one[64 * c : 64 * c + 64] for one in taken], axis=0)
                for c in range(2)
            ]
            blocks = [dot(perm_t[...], block).astype(BF) for block in blocks]
            gparts[:, :, :, :, lanes] = jnp.concatenate(blocks, axis=0).reshape(
                RING, RING, 2, 2 * CAP, 512
            )
            return carry

        lax.fori_loop(0, half_width // 512, sort_out, 0)

        grad_stream = scatter(
            links, halves, gparts, grad_land, grad_base
        )
        next(grad_stream)
        expert()
        drive([scatter(links, halves, parts, ret_land, ret_base), grad_stream])
        grad_out[...] = scattered(gparts, (x, y, z), grad_land)
        finish(resid)
        keep(resid).wait()
        links.finish()


def place_rows(
    base, before, own_rows, their_rows, own_slot, their_slot, grad, layer_out, arriving, grad_out
):
    upper = pl.program_id(0) >= pl.num_programs(0) // 2
    tokens, lanes = base.shape
    row = lax.broadcasted_iota(jnp.int32, (2 * CAP, tokens), 0) - jnp.where(upper, CAP, 0)
    for slots, rows, kept, target in (
        (own_slot[:1, :], own_rows, base, layer_out),
        (their_slot[:1, :], their_rows, before, arriving),
    ):
        chosen = jnp.where(row < 0, 0.0, (slots == row).astype(F32)).astype(BF)
        turned = chosen.astype(F32).T.astype(BF)
        free = (1.0 - jnp.sum(turned.astype(F32), axis=-1, keepdims=True)).astype(BF)
        for start in range(0, lanes, 256):
            part = slice(start, start + 256)
            moved = dot(turned, rows[:, part]).astype(BF)
            target[:, part] = moved + kept[:, part] * free
    total = jnp.where(upper, grad[CAP:, :], grad[:CAP, :])
    for r in range(grad_out.shape[0]):
        grad_out[r] = total[2 * r : 2 * r + 2]


def local(
    layer_in, memory, cotangent, norm_gain, attn_gain, expert_in, expert_out, slot_index, gate_prob
):
    sections = lax.axis_size("section")
    tokens, width = layer_in.shape[1:]
    rows = memory.shape[1]
    stash = rows * 2 * RING * RING
    ffw = expert_in.shape[2]
    half = width // 2
    heads = width // HD
    vmem = pl.BlockSpec(memory_space=pltpu.VMEM)
    anywhere = pl.BlockSpec(memory_space=pl.ANY)
    full = (RING, RING, 2, 2 * CAP, half)
    quarter = half // 4
    landing = [
        pltpu.VMEM((2, RING, 2, 2, 2 * CAP, quarter), BF),
        pltpu.VMEM((2, RING, 2, 2, 2 * CAP, 2 * quarter), BF),
        pltpu.VMEM((2, len(GROUP), 2 * CAP, 2 * quarter), BF),
    ]
    count = 2 * GATHER_KEYS + 2 * SCATTER_KEYS + PIECES + 2
    base, before, own_rows, their_rows, their_slot, grad = pl.pallas_call(
        lambda *refs: kernel(sections, *refs),
        out_shape=(
            jax.ShapeDtypeStruct((tokens, width), BF),
            jax.ShapeDtypeStruct((tokens, width), BF),
            jax.ShapeDtypeStruct((2 * CAP, half), BF),
            jax.ShapeDtypeStruct((2 * CAP, half), BF),
            jax.ShapeDtypeStruct((8, tokens), jnp.int32),
            jax.ShapeDtypeStruct((2 * CAP, half), F32),
        ),
        in_specs=[vmem, anywhere, anywhere, vmem, vmem, anywhere, anywhere, vmem, vmem],
        out_specs=(anywhere, anywhere, vmem, vmem, vmem, vmem),
        scratch_shapes=[
            pltpu.VMEM((tokens, width), BF),
            pltpu.VMEM((tokens, width), BF),
            pltpu.VMEM((ffw, width), BF),
            pltpu.VMEM((ffw, width), BF),
            pltpu.VMEM((tokens, width), BF),
            pltpu.VMEM((tokens, width), BF),
            pltpu.VMEM(full, BF),
            pltpu.VMEM((stash, width), BF),
            pltpu.VMEM((stash, width), BF),
            pltpu.VMEM(full, BF),
            pltpu.VMEM((heads, stash, tokens), F32),
            pltpu.VMEM(full, BF),
            pltpu.VMEM(full, BF),
            pltpu.VMEM((stash, width), BF),
            pltpu.VMEM((stash, width), BF),
            pltpu.VMEM((2 * CAP, width), BF),
            pltpu.VMEM((2 * CAP, width), BF),
            pltpu.VMEM((2 * CAP, width), F32),
            pltpu.VMEM((256, 256), BF),
            pltpu.VMEM((256, 256), BF),
            pltpu.VMEM((ffw, 2 * RING * RING * CAP), F32),
            pltpu.VMEM((2 * RING * RING * CAP, ffw), BF),
            pltpu.VMEM((8, tokens), jnp.int32),
            *landing,
            *landing,
            pltpu.SemaphoreType.DMA((6,)),
            pltpu.SemaphoreType.DMA((count,)),
            pltpu.SemaphoreType.DMA((count,)),
        ],
        compiler_params=pltpu.CompilerParams(
            collective_id=0, has_side_effects=True, vmem_limit_bytes=60 * 1024 * 1024
        ),
    )(
        memory[0],
        layer_in[0],
        cotangent[0],
        norm_gain,
        attn_gain,
        expert_in[0].T,
        expert_out[0],
        slot_index,
        gate_prob,
    )
    steps = 2
    lanes = width // steps
    whole = pl.BlockSpec((tokens, lanes), lambda i: (0, i))
    folded = pl.BlockSpec((2 * CAP, lanes), lambda i: (0, i % (steps // 2)))
    layer_out, arriving, grad_memory = pl.pallas_call(
        place_rows,
        grid=(steps,),
        out_shape=(
            jax.ShapeDtypeStruct((tokens, width), BF),
            jax.ShapeDtypeStruct((tokens, width), BF),
            jax.ShapeDtypeStruct((rows, 2, width), F32),
        ),
        in_specs=[
            whole,
            whole,
            folded,
            folded,
            pl.BlockSpec((1, tokens), lambda i: (0, 0)),
            pl.BlockSpec((8, tokens), lambda i: (0, 0)),
            folded,
        ],
        out_specs=(whole, whole, pl.BlockSpec((rows, 2, lanes), lambda i: (0, 0, i))),
    )(base, before, own_rows, their_rows, slot_index, their_slot, grad)
    return (layer_out[None], arriving[None], grad_memory[None])


def solution(mesh):
    placed = (
        P("section", "expert", None),
        P("section", "expert", None, None),
        P("section", "expert", None),
        P("section", None),
        P("section", None),
        P("section", None, "expert"),
        P("section", "expert", None),
        P("section", "expert"),
        P("section", "expert"),
    )
    return jax.shard_map(
        local,
        mesh=mesh,
        in_specs=placed,
        out_specs=(
            P("section", "expert", None),
            P("section", "expert", None),
            P("section", "expert", None, None),
        ),
        check_vma=False,
    )
```
